128 devices in a mesh: blk: 64 (over x, y, z_lo, core), rep: 2 (over z_hi).
Axes of the slice: x: 4, y: 4, z: 4 (z_hi: 2, z_lo: 2; z = z_hi * 2 + z_lo), core: 2. Of those that a mesh axis runs over, the one named last changes fastest.
Arguments:
- points: bfloat16 [64, 49152], P(None, ('blk', 'rep')), may hold values from -6 to 6
- targets: float32 [32, 49152], P(None, ('blk', 'rep')), may hold values from -15 to 15
- cal_offset: int32 [16384], P(('blk', 'rep')), may hold values from 0 to 383
Outputs:
- coefficients: float32 [32, 49152], P(None, ('blk', 'rep'))
- residual: float32 [32, 49152], P(None, ('blk', 'rep'))
- scores: float32 [32, 16384], P(None, ('blk', 'rep'))
The draws below stay inside these ranges and needn't reach their ends.
All inputs are finite; a program needn't handle non-finite values.
Results may differ from the reference program's by a relative error of at most 0.0008.
Values may be sent and summed in bfloat16 or wider, within the bound.
No kernel may reach another device: no remote copies, remote signals or barrier semaphores. Data moves between devices by JAX's collectives and lax.ppermute only.
A program may use at most 64 MiB of HBM per device.

```python
import jax
import jax.numpy as jnp
from jax import lax

EMBED = 64
SIDES = 32
POINTS_DEV = 384
CALIB_DEV = 128
ITERATIONS = 3
POINTS = 49152
CALIB = 16384
N_BLK = 64
N_REP = 2


def draw_targets(key, part):
    key = jax.random.fold_in(key, 7)
    position = jnp.arange(POINTS, dtype=jnp.float32) / POINTS
    noise = jnp.clip(jax.random.normal(key, (SIDES, POINTS), jnp.float32), -5.0, 5.0)
    return noise * (1.0 + 2.0 * position)[None, :]


def place_ends(values, stream_key, smallest, top_value):
    index_at = [jax.random.randint(jax.random.fold_in(stream_key, axis), (), 0, length) for axis, length in enumerate(values.shape)]
    longest = values.shape.index(max(values.shape))
    neighbour = index_at[:longest] + [(index_at[longest] + 1) % values.shape[longest]] + index_at[longest + 1:]
    return values.at[tuple(index_at)].set(smallest).at[tuple(neighbour)].set(top_value)


def block_levels(stream_key, extent, shards, least, top_value):
    factor_of, own = 1.0, jax.random.fold_in(stream_key, 6)
    for dim, blocks in shards:
        draws = jnp.exp(jax.random.uniform(jax.random.fold_in(own, dim), (blocks,), jnp.float32, least / len(shards), top_value / len(shards)))
        factor_of = factor_of * jnp.repeat(draws, extent[dim] // blocks).reshape([-1 if axis == dim else 1 for axis in range(len(extent))])
    return factor_of


def centred(rng, dims, deviation, most, shards=(), kind=jnp.bfloat16):
    entries = jax.random.normal(rng, dims, jnp.float32) * deviation
    if len(shards) > 0:
        entries = block_levels(rng, dims, shards, -0.22, 0.18) * entries
    return jnp.clip(entries, min=-most, max=most).astype(kind)


def setup_inputs(seed: int = 0) -> dict:
    keys = jax.random.split(jax.random.key(seed), 4)
    return {
        "points": centred(keys[0], (EMBED, POINTS), 1.0, 6.0, ((1, 128),)),
        "targets": draw_targets(jax.random.fold_in(keys[3], 71), 0),
        "cal_offset": place_ends(jax.random.randint(keys[2], (CALIB,), 0, POINTS_DEV), jax.random.fold_in(keys[2], 1), 0, POINTS_DEV - 1).astype(jnp.int32),
    }


shrinkage = 0.5


def kernel_tile(row_points, col_points, sharpness):
    row_sq = jnp.sum(jnp.square(row_points.astype(jnp.float32)), axis=0)
    col_sq = jnp.sum(jnp.square(col_points.astype(jnp.float32)), axis=0)
    inner_products = lax.dot_general(row_points, col_points, (((0,), (0,)), ((), ())), preferred_element_type=jnp.float32)
    distance = row_sq[:, None] + col_sq[None, :] - 2.0 * inner_products
    return jnp.exp(-sharpness * distance)


def apply_operator(points, vectors):
    sharpness = 3.0 / points.shape[0]
    block_rows = POINTS_DEV * N_REP
    blocks = jnp.transpose(points.reshape(points.shape[0], N_BLK, block_rows), (1, 0, 2))

    def one_block(row_points):
        tile_values = kernel_tile(row_points, points, sharpness)
        return lax.dot_general(vectors, tile_values, (((1,), (1,)), ((), ())), precision=lax.Precision.HIGHEST, preferred_element_type=jnp.float32)

    products = lax.map(one_block, blocks)
    products = jnp.transpose(products, (1, 0, 2)).reshape(vectors.shape[0], -1)
    return products + shrinkage * vectors


def reference(points, targets, cal_offset):
    coefficients = jnp.zeros_like(targets)
    residual, direction = targets, targets
    norm_now = jnp.sum(residual * residual, axis=1)
    for iteration in range(ITERATIONS):
        mapped = apply_operator(points, direction)
        step_size = norm_now / jnp.sum(direction * mapped, axis=1)
        coefficients = coefficients + step_size[:, None] * direction
        residual = residual - step_size[:, None] * mapped
        norm_next = jnp.sum(residual * residual, axis=1)
        direction = residual + (norm_next / norm_now)[:, None] * direction
        norm_now = norm_next
    values = residual + shrinkage * coefficients
    owners = (jnp.arange(CALIB, dtype=jnp.int32) // CALIB_DEV) * POINTS_DEV
    positions = (owners + cal_offset).astype(jnp.int32)
    scores = jnp.abs(jnp.take(values, positions, axis=1))
    return coefficients, residual, scores
```

```python
import functools

import jax
import jax.numpy as jnp
from jax import lax
from jax.experimental import pallas as pl
from jax.experimental.pallas import tpu as pltpu
from jax.sharding import Mesh, PartitionSpec as P

ALL = ("x", "y", "zl", "c", "zh")
Z = ("zl", "zh")
BF16, F32, F8 = jnp.bfloat16, jnp.float32, jnp.float8_e4m3fn
SHRINKAGE = 0.5
LOG2E = 1.4426950408889634
LOW_SCALE = 2.0**17
VM = pl.BlockSpec(memory_space=pltpu.VMEM)
SIDES, WIDTH, LANES = 32, 384, 128


def call(kernel, outs, limit, scratch=(), cost=None, name=None):
    return lambda *args: pl.pallas_call(
        kernel,
        out_shape=outs,
        in_specs=[VM] * len(args),
        out_specs=[VM] * len(outs),
        scratch_shapes=scratch,
        compiler_params=pltpu.CompilerParams(vmem_limit_bytes=limit),
        cost_estimate=cost,
        name=name,
    )(*args)


def f32(*shape):
    return jax.ShapeDtypeStruct(shape, F32)


def swap(array, axis, k, size=4):
    return lax.ppermute(array, axis, [(i, i ^ k) for i in range(size)])


def round_of(array, axis):
    return [array] + [swap(array, axis, k) for k in (1, 3, 2)]


def split3(a):
    first = a.astype(BF16)
    rest = a - first.astype(F32)
    second = rest.astype(BF16)
    return first, second, (rest - second.astype(F32)).astype(BF16)


def tail_rows(first, second, n):
    rows = [part.astype(F32) for part in (*first, *second)]
    return jnp.concatenate([*rows, jnp.zeros((10, n), F32)], axis=0).astype(BF16)


def form_kernel(rows, sharpness, xj_ref, xi_ref, hi_ref, lo_ref, right, left_t, left):
    count, columns = xj_ref.shape[1], xi_ref.shape[1]
    xi = xi_ref[...].astype(F32)
    sq_i = jnp.sum(xi * xi, axis=0, keepdims=True) * (-sharpness * LOG2E)
    for place, part in enumerate(split3(xi * (2.0 * sharpness * LOG2E))):
        right[place * 64 : place * 64 + 64, :] = part
    ones = [jnp.ones((1, columns), F32)] * 3
    right[192:208, :] = tail_rows(split3(sq_i), ones, columns)
    right[208:256, :] = jnp.zeros((48, columns), BF16)
    xj = xj_ref[...]
    xf = xj.astype(F32)
    sq_j = jnp.sum(xf * xf, axis=0, keepdims=True) * (-sharpness * LOG2E)
    for place in range(3):
        left_t[place * 64 : place * 64 + 64, :] = xj
    ones = [jnp.ones((1, count), F32)] * 3
    left_t[192:208, :] = tail_rows(ones, split3(sq_j), count)
    left_t[208:256, :] = jnp.zeros((48, count), BF16)

    @pl.loop(0, count // 128)
    def _(r):
        at = pl.ds(pl.multiple_of(r * 128, 128), 128)
        left[at, :] = left_t[:, at].T

    @pl.loop(0, count // rows)
    def _(r):
        at = pl.ds(pl.multiple_of(r * rows, rows), rows)
        part = left[at, :]
        for c in range(columns // 256):
            cols = slice(c * 256, c * 256 + 256)
            value = jnp.exp2(jnp.dot(part, right[:, cols], preferred_element_type=F32))
            high = value.astype(BF16)
            hi_ref[at, cols] = high
            lo_ref[at, cols] = ((value - high.astype(F32)) * LOW_SCALE).astype(F8)


def form(xj, xi):
    count, columns = xj.shape[1], xi.shape[1]
    sharpness = 3.0 / xj.shape[0]
    return call(
        functools.partial(form_kernel, 128, sharpness),
        [pltpu.VMEM((count, columns), BF16), pltpu.VMEM((count, columns), F8)],
        8 * 2**20,
        [pltpu.VMEM((256, columns), BF16), pltpu.VMEM((256, count), BF16), pltpu.VMEM((count, 256), BF16)],
        name="form",
    )(xj, xi)


def total(a):
    return jnp.sum(a, axis=1, keepdims=True)


def in_lanes(*values):
    lane = lax.broadcasted_iota(jnp.int32, (SIDES, LANES), 1)
    tile = jnp.zeros((SIDES, LANES), F32)
    for place, value in enumerate(values):
        tile = jnp.where(lane == place, value, tile)
    return tile


def sums_first(v):
    return (total(v * v),)


def sums_second(v, b):
    return total(b * v), total(v * v)


def sums_third(v, b, u0, coef):
    r1 = b - coef[:, 0:1] * u0
    d1 = r1 + coef[:, 1:2] * b
    return total(d1 * v), total(v * v), total(r1 * v), total(r1 * r1)


def apply_kernel(sums, begin, end, n_extra, *refs):
    v_ref, *refs = refs
    extra, refs = refs[:n_extra], refs[n_extra:]
    hi_ref, lo_ref, *refs = refs
    if not begin:
        acc_ref, *refs = refs
    parts = refs[-1]
    outs = refs[:-1]
    v = v_ref[...]
    for place, part in enumerate(split3(v)):
        parts[place * SIDES : place * SIDES + SIDES, :] = part
    tile = in_lanes(*sums(v, *[e[...] for e in extra]))
    columns = hi_ref.shape[1]
    if not begin:
        tile = tile + acc_ref[:, columns:]
    for c in range(columns // 256):
        cols = slice(c * 256, c * 256 + 256)
        a = jnp.dot(parts[...], hi_ref[:, cols], preferred_element_type=F32)
        b = jnp.dot(parts[0 : 2 * SIDES, :], lo_ref[:, cols], preferred_element_type=F32)
        low = (b[0:SIDES] + b[SIDES:]) * (1.0 / LOW_SCALE)
        value = a[0:SIDES] + (a[SIDES : 2 * SIDES] + (low + a[2 * SIDES :]))
        if not begin:
            value = value + acc_ref[:, cols]
        if not end:
            outs[0][:, cols] = value
            continue
        for half in range(2):
            m, at = divmod(c * 256 + half * 128, WIDTH)
            outs[m][:, at : at + 128] = value[:, half * 128 : half * 128 + 128]
    if end:
        for out in outs:
            out[:, WIDTH:] = tile
    else:
        outs[0][:, columns:] = tile


def apply_part(sums, begin, end, v, extra, hi, lo, acc):
    columns = hi.shape[1]
    outs = [f32(SIDES, WIDTH + LANES)] * 4 if end else [f32(SIDES, columns + LANES)]
    got = call(
        functools.partial(apply_kernel, sums, begin, end, len(extra)),
        outs,
        6 * 2**20,
        [pltpu.VMEM((3 * SIDES, v.shape[1]), BF16)],
        name="apply",
    )(v, *extra, hi, lo, *([] if begin else [acc]))
    return got if end else got[0]


def product(sums, vectors, extras, blocks, common=()):
    acc = None
    last = len(vectors) - 1
    for k, (hi, lo) in enumerate(blocks):
        extra = [e[k] for e in extras] + list(common)
        acc = apply_part(sums, k == 0, k == last, vectors[k], extra, hi, lo, acc)
    return [acc[0]] + [swap(acc[m], Z, m) for m in (1, 3, 2)]


def gather_plane(array):
    rows = jnp.concatenate(round_of(array, "y"), axis=1)
    planes = round_of(rows, "x")
    return [jnp.concatenate([p, swap(p, "c", 1, 2)], axis=1) for p in planes]


def added(refs):
    got = (refs[0][...] + refs[1][...]) + (refs[2][...] + refs[3][...])
    return got[:, :WIDTH], got[:, WIDTH:]


def first_kernel(m0, m1, m2, m3, b_ref, u_ref, sums_ref):
    got, sums_ref[...] = added((m0, m1, m2, m3))
    u_ref[...] = got + SHRINKAGE * b_ref[...]


def second_kernel(m0, m1, m2, m3, b_ref, u0_ref, sums_ref, u1_ref, r1_ref, d1_ref, ar1_ref, coef_ref):
    got, sums = added((m0, m1, m2, m3))
    b, u0 = b_ref[...], u0_ref[...]
    y = got + SHRINKAGE * u0
    rr0, c0, q0 = sums_ref[:, 0:1], sums[:, 0:1], sums[:, 1:2]
    a0 = rr0 / c0
    rr1 = rr0 - 2.0 * a0 * c0 + a0 * a0 * q0
    b0 = rr1 / rr0
    r1 = b - a0 * u0
    ar1 = u0 - a0 * y
    r1_ref[...] = r1
    d1_ref[...] = r1 + b0 * b
    ar1_ref[...] = ar1
    u1_ref[...] = ar1 + b0 * u0
    coef_ref[...] = in_lanes(a0, b0)


def third_kernel(
    m0, m1, m2, m3, b_ref, u1_ref, r1_ref, d1_ref, ar1_ref, coef_ref, x2_ref, r2_ref, d2_ref, u2_ref, sums_ref
):
    got, sums = added((m0, m1, m2, m3))
    u1, d1, r1 = u1_ref[...], d1_ref[...], r1_ref[...]
    y = got + SHRINKAGE * u1
    c1, q1, p1, rr1 = (sums[:, k : k + 1] for k in range(4))
    a1 = rr1 / c1
    rr2 = rr1 - 2.0 * a1 * p1 + a1 * a1 * q1
    b1 = rr2 / rr1
    r2 = r1 - a1 * u1
    d2 = r2 + b1 * d1
    u2 = (ar1_ref[...] - a1 * y) + b1 * u1
    x2_ref[...] = coef_ref[:, 0:1] * b_ref[...] + a1 * d1
    r2_ref[...] = r2
    d2_ref[...] = d2
    u2_ref[...] = u2
    tile = jnp.concatenate([in_lanes(total(d2 * u2), total(r2 * r2)), jnp.zeros((LANES - SIDES, LANES), F32)], axis=0)
    sums_ref[...] = jnp.transpose(tile)[0:8, :]


def last_kernel(sums_ref, x2_ref, r2_ref, d2_ref, u2_ref, at_ref, x_ref, r_ref, s_ref):
    got = jnp.transpose(jnp.sum(sums_ref[...], axis=0))[0:SIDES, :]
    a2 = got[:, 1:2] / got[:, 0:1]
    x = x2_ref[...] + a2 * d2_ref[...]
    r = r2_ref[...] - a2 * u2_ref[...]
    x_ref[...] = x
    r_ref[...] = r
    place = lax.broadcasted_iota(jnp.int32, (WIDTH, LANES), 0)
    pick = jnp.where(place == at_ref[...], 1.0, 0.0).astype(BF16)
    parts = [jnp.dot(p, pick, preferred_element_type=F32) for p in split3(r + SHRINKAGE * x)]
    s_ref[...] = jnp.abs((parts[0] + parts[1]) + parts[2])


def body(points, targets, cal_offset):
    small = 4 * 2**20
    vector = f32(SIDES, WIDTH)
    tile = f32(SIDES, LANES)
    xi = jnp.concatenate([points] + [swap(points, Z, m) for m in (1, 2, 3)], axis=1)
    blocks = [form(xj, xi) for xj in gather_plane(points)]
    b = targets
    bj = gather_plane(b)
    msgs = product(sums_first, bj, [], blocks)
    u0, sums = call(first_kernel, [vector, tile], small, name="first")(*msgs, b)
    u0j = gather_plane(u0)
    msgs = product(sums_second, u0j, [bj], blocks)
    u1, r1, d1, ar1, coef = call(second_kernel, [vector] * 4 + [tile], small, name="second")(*msgs, b, u0, sums)
    msgs = product(sums_third, gather_plane(u1), [bj, u0j], blocks, (coef,))
    x2, r2, d2, u2, part = call(third_kernel, [vector] * 4 + [f32(8, LANES)], small, name="third")(
        *msgs, b, u1, r1, d1, ar1, coef
    )
    parts = lax.all_to_all(
        jnp.broadcast_to(part[None], (128, 8, LANES)), ALL, split_axis=0, concat_axis=0, tiled=True
    )
    return tuple(
        call(last_kernel, [vector, vector, tile], small, name="last")(
            parts, x2, r2, d2, u2, cal_offset.reshape(1, LANES)
        )
    )


def solution(mesh):
    grid = Mesh(mesh.devices.reshape(4, 4, 2, 2, 2), ALL)
    return jax.shard_map(
        body,
        mesh=grid,
        in_specs=(P(None, ALL), P(None, ALL), P(ALL)),
        out_specs=(P(None, ALL), P(None, ALL), P(None, ALL)),
        check_vma=False,
    )
```

```python
import functools

import jax
import jax.numpy as jnp
from jax import lax
from jax.experimental import pallas as pl
from jax.experimental.pallas import tpu as pltpu
from jax.sharding import Mesh, PartitionSpec as P

ALL = ("x", "y", "zl", "c", "zh")
Z = ("zl", "zh")
BF16, F32, F8 = jnp.bfloat16, jnp.float32, jnp.float8_e4m3fn
SHRINKAGE = 0.5
LOG2E = 1.4426950408889634
VM = pl.BlockSpec(memory_space=pltpu.VMEM)
HB = pl.BlockSpec(memory_space=pltpu.HBM)
TILE, ROWS, DEPTH = 512, 64, 4
NEAR, KEEP = (1, 1, 1, 5), 2
FORM_ROOM, APPLY_ROOM = 3 * 2**20, 1 * 2**20
SIDES, WIDTH, LANES = 32, 384, 128


def call(kernel, outs, limit, scratch=(), cost=None, in_specs=None, out_specs=None, name=None):
    if cost is not None:
        cost = pl.CostEstimate(flops=0, transcendentals=0, bytes_accessed=int(cost * 3.6e6))
    return lambda *args: pl.pallas_call(
        kernel,
        out_shape=outs,
        in_specs=in_specs or [VM] * len(args),
        out_specs=out_specs or [VM] * len(outs),
        scratch_shapes=scratch,
        compiler_params=pltpu.CompilerParams(vmem_limit_bytes=limit),
        cost_estimate=cost,
        name=name,
    )(*args)


def f32(*shape):
    return jax.ShapeDtypeStruct(shape, F32)


def swap(array, axis, k, size=4):
    return lax.ppermute(array, axis, [(i, i ^ k) for i in range(size)])


def round_of(array, axis):
    return [array] + [swap(array, axis, k) for k in (1, 3, 2)]


def split3(a):
    first = a.astype(BF16)
    rest = a - first.astype(F32)
    second = rest.astype(BF16)
    return first, second, (rest - second.astype(F32)).astype(BF16)


def tail_rows(first, second, n):
    rows = [part.astype(F32) for part in (*first, *second)]
    return jnp.concatenate([*rows, jnp.zeros((10, n), F32)], axis=0).astype(BF16)


def pack_kernel(points_ref, targets_ref, out_ref, targets, sems):
    copies = [
        pltpu.make_async_copy(points_ref, out_ref.at[0:64, :], sems.at[0]),
        pltpu.make_async_copy(targets_ref, targets, sems.at[1]),
    ]
    for copy in copies:
        copy.start()
    copies[1].wait()
    for place, part in enumerate(split3(targets[...])):
        out_ref[64 + place * SIDES : 64 + place * SIDES + SIDES, :] = part
    copies[0].wait()


def unpacked(ref):
    parts = [ref[64 + place * SIDES : 64 + place * SIDES + SIDES, :].astype(F32) for place in range(3)]
    return (parts[0] + parts[1]) + parts[2]


def prepare_kernel(sharpness, xi_ref, right):
    columns = xi_ref.shape[1]
    xi = xi_ref[...].astype(F32)
    sq = jnp.sum(xi * xi, axis=0, keepdims=True) * (-sharpness * LOG2E)
    for place, part in enumerate(split3(xi * (2.0 * sharpness * LOG2E))):
        right[place * 64 : place * 64 + 64, :] = part
    ones = [jnp.ones((1, columns), F32)] * 3
    right[192:208, :] = tail_rows(split3(sq), ones, columns)
    right[208:256, :] = jnp.zeros((48, columns), BF16)


def form_kernel(sharpness, kind, near, *refs):
    pack_ref, right, *refs = refs
    acc_ref, refs = (None, refs) if kind == "first" else (refs[0], refs[1:])
    tiles = right.shape[1] // TILE
    hi_refs, refs = refs[:tiles], refs[tiles:]
    near_refs, refs = refs[:near], refs[near:]
    far_ref, refs = (refs[0], refs[1:]) if near < tiles else (None, refs)
    out_ref, left_t, left, *own = refs
    if far_ref is not None:
        stage, sems = own
    count = pack_ref.shape[1]
    xj = pack_ref[0:64, :]
    xf = xj.astype(F32)
    sq = jnp.sum(xf * xf, axis=0, keepdims=True) * (-sharpness * LOG2E)
    for place in range(3):
        left_t[place * 64 : place * 64 + 64, :] = xj
    ones = [jnp.ones((1, count), F32)] * 3
    left_t[192:208, :] = tail_rows(ones, split3(sq), count)
    left_t[208:256, :] = jnp.zeros((48, count), BF16)
    for r in range(count // 128):
        at = slice(r * 128, r * 128 + 128)
        left[at, :] = left_t[:, at].T
    finish_tile(kind, sums_first, unpacked(pack_ref), (), acc_ref, None, out_ref)

    def copy(c, slot):
        return pltpu.make_async_copy(stage.at[slot], far_ref.at[c - near], sems.at[slot])

    def step(units, c, slot):
        starts = [pl.multiple_of(c * TILE + m * 256, 256) for m in range(2)]
        lows = near_refs[c] if slot is None else stage.at[slot]

        def finish(at, m, value):
            value = jnp.exp2(value)
            high = value.astype(BF16)
            hi_refs[c][at, m * 256 : m * 256 + 256] = high
            lows[at, m * 256 : m * 256 + 256] = (value - high.astype(F32)).astype(BF16)

        for m in range(2):
            pltpu.matmul_push_rhs(right[:, pl.ds(starts[m], 256)], 0, m)
        waiting = []
        for r in range(count // ROWS):
            at = slice(r * ROWS, r * ROWS + ROWS)
            for m in range(2):
                unit = units[m][r % DEPTH]
                pltpu.matmul_acc_lhs(unit, left[at, :], load_staged_rhs=0 if r == 0 else None)
                waiting.append((at, m, unit))
            if len(waiting) > 2 * (DEPTH - 1):
                for _ in range(2):
                    at, m, unit = waiting.pop(0)
                    finish(at, m, pltpu.matmul_pop(unit))
        for at, m, unit in waiting:
            finish(at, m, pltpu.matmul_pop(unit))
        turn = 0
        for k in range(count // 256):
            rows = slice(k * 256, k * 256 + 256)
            for source, which, height in ((hi_refs[c], -2, 96), (lows, -1, 64)):
                for m in range(2):
                    pltpu.matmul_push_rhs(source[rows, m * 256 : m * 256 + 256], turn % 2, m)
                for m in range(2):
                    pltpu.matmul_acc_lhs(units[m][which], pack_ref[64 : 64 + height, rows], load_staged_rhs=turn % 2)
                turn += 1
        for m in range(2):
            a, b = pltpu.matmul_pop(units[m][-2]), pltpu.matmul_pop(units[m][-1])
            value = a[0:SIDES] + (a[SIDES : 2 * SIDES] + ((b[0:SIDES] + b[SIDES:]) + a[2 * SIDES :]))
            if acc_ref is not None:
                value = value + acc_ref[:, pl.ds(starts[m], 256)]
            out_ref[:, pl.ds(starts[m], 256)] = value

    def steps(*units):
        each = len(units) // 2
        units = (units[:each], units[each:])
        for c in range(near, tiles):
            slot = (c - near) % KEEP
            if c >= near + KEEP:
                copy(c - KEEP, slot).wait()
            step(units, c, slot)
            copy(c, slot).start()
        for c in range(near):
            step(units, c, None)
        for c in range(max(near, tiles - KEEP), tiles):
            copy(c, (c - near) % KEEP).wait()

    heights = [ROWS] * DEPTH + [96, 64]
    pl.run_scoped(steps, *[pltpu.ACC(m)((h, 256), F32) for m in range(2) for h in heights])


def finish_tile(kind, sums, v, extra, acc_ref, tile_ref, out_ref):
    width = out_ref.shape[1] - LANES
    if kind == "own":
        tile = tile_ref[:, tile_ref.shape[1] - LANES :]
    else:
        tile = in_lanes(*sums(v, *extra))
        if acc_ref is not None:
            tile = tile + acc_ref[:, acc_ref.shape[1] - LANES :]
    out_ref[:, width:] = tile


def form(kind, near, pack, right, acc):
    count, width = pack.shape[1], right.shape[1]
    tiles = width // TILE
    outs = [pltpu.VMEM((count, TILE), BF16)] * (tiles + near)
    specs = [VM] * (tiles + near)
    scratch = [pltpu.VMEM((256, count), BF16), pltpu.VMEM((count, 256), BF16)]
    keep = min(KEEP, tiles - near)
    if keep:
        outs.append(pltpu.HBM((tiles - near, count, TILE), BF16))
        specs.append(HB)
        scratch += [pltpu.VMEM((keep, count, TILE), BF16), pltpu.SemaphoreType.DMA((keep,))]
    *parts, out = call(
        functools.partial(form_kernel, 3.0 / 64, kind, near),
        outs + [f32(SIDES, width + LANES)],
        FORM_ROOM + 3 * 2**19 * keep,
        scratch,
        cost=8.5,
        out_specs=specs + [VM],
        name="form",
    )(pack, right, *acc)
    return (parts[:tiles], parts[tiles : tiles + near], parts[tiles + near :]), out


def apply_kernel(sums, kind, columns, n_extra, all_tiles, near, *refs):
    v_ref, *refs = refs
    extra, refs = refs[:n_extra], refs[n_extra:]
    hi_refs, refs = refs[:all_tiles], refs[all_tiles:]
    near_refs, refs = refs[:near], refs[near:]
    far_ref, refs = (refs[0], refs[1:]) if near < all_tiles else (None, refs)
    acc_ref, refs = (None, refs) if kind == "first" else (refs[0], refs[1:])
    tile_ref, refs = (refs[0], refs[1:]) if kind == "own" else (None, refs)
    out_ref, parts, *own = refs
    if own:
        slots, sems = own
    tiles = range(columns // TILE, (columns + out_ref.shape[1] - LANES) // TILE)
    far_tiles = [c for c in tiles if c >= near]

    def copy(c):
        slot = c - far_tiles[0]
        return pltpu.make_async_copy(far_ref.at[c - near], slots.at[slot], sems.at[slot])

    for c in far_tiles:
        copy(c).start()
    v = v_ref[...]
    for place, part in enumerate(split3(v)):
        parts[place * SIDES : place * SIDES + SIDES, :] = part
    for c in tiles:
        cols, from_cols = (slice(at, at + TILE) for at in (c * TILE - columns, c * TILE))
        a = jnp.dot(parts[...], hi_refs[c][...], preferred_element_type=F32)
        value = a[0:SIDES] + (a[SIDES : 2 * SIDES] + a[2 * SIDES :])
        if acc_ref is not None:
            value = value + acc_ref[:, from_cols]
        out_ref[:, cols] = value
    finish_tile(kind, sums, v, extra, acc_ref, tile_ref, out_ref)
    for c in tiles:
        cols, from_cols = (slice(at, at + TILE) for at in (c * TILE - columns, c * TILE))
        if c >= near:
            copy(c).wait()
            low = slots[c - far_tiles[0]]
        else:
            low = near_refs[c][...]
        b = jnp.dot(parts[0 : 2 * SIDES, :], low, preferred_element_type=F32)
        out_ref[:, cols] = out_ref[:, cols] + (b[0:SIDES] + b[SIDES:])


def apply_block(sums, kind, columns, width, v, extra, hi, near, far, acc, tile):
    count = hi[0].shape[0]
    slots = sum(c >= len(near) for c in range(columns // TILE, (columns + width) // TILE))
    scratch = [pltpu.VMEM((3 * SIDES, count), BF16)]
    if slots:
        scratch += [pltpu.VMEM((slots, count, TILE), BF16), pltpu.SemaphoreType.DMA((slots,))]
    args, specs = [v, *extra, *hi], [VM] * (1 + len(extra) + len(hi))
    args += [*near, *[pltpu.with_memory_space_constraint(array, pltpu.HBM) for array in far]]
    specs += [VM] * len(near) + [HB] * len(far)
    return call(
        functools.partial(apply_kernel, sums, kind, columns, len(extra), len(hi), len(near)),
        [f32(SIDES, width + LANES)],
        APPLY_ROOM + 3 * 2**19 * slots,
        scratch,
        cost=(4.4 if slots else 3.2) * width / 3072,
        in_specs=specs + [VM] * len(acc + tile),
        name="apply",
    )(*args, *acc, *tile)[0]


def summed(own, other):
    fold = call(fold_kernel, [f32(SIDES, WIDTH + LANES)] * 4, 2**20, name="fold")
    parts = fold(own, swap(other, "c", 1, 2))
    return [parts[0]] + [swap(parts[m], Z, m) for m in (1, 3, 2)]


def first_product(packs, right):
    blocks, acc = [], []
    for k, pack in enumerate(packs):
        block, out = form("next" if k else "first", NEAR[k], pack, right, acc)
        blocks.append(block)
        acc = [out]
    half = 4 * WIDTH
    halves = [jnp.concatenate([out[:, at : at + half], out[:, 2 * half :]], axis=1) for at in (0, half)]
    return summed(*halves), blocks


def product(sums, vectors, extras, blocks, common=()):
    half, last = 4 * WIDTH, len(vectors) - 1

    def work(kind, k, columns, width, acc, tile):
        extra = [e[k] for e in extras] + list(common)
        return apply_block(sums, kind, columns, width, vectors[k], extra, *blocks[k], acc, tile)

    acc = []
    for k in range(last):
        acc = [work("next" if k else "first", k, 0, 2 * half, acc, [])]
    other = work("other", last, half, half, acc, [])
    return summed(work("own", last, 0, half, acc, [other]), other)


def fold_kernel(own_ref, got_ref, *outs):
    value = own_ref[...] + got_ref[...]
    for m, out in enumerate(outs):
        out[:, :WIDTH] = value[:, m * WIDTH : m * WIDTH + WIDTH]
        out[:, WIDTH:] = value[:, 4 * WIDTH :]


def total(a):
    return jnp.sum(a, axis=1, keepdims=True)


def in_lanes(*values):
    lane = lax.broadcasted_iota(jnp.int32, (SIDES, LANES), 1)
    tile = jnp.zeros((SIDES, LANES), F32)
    for place, value in enumerate(values):
        tile = jnp.where(lane == place, value, tile)
    return tile


def sums_first(v):
    return (total(v * v),)


def sums_second(v, b_ref):
    return total(unpacked(b_ref) * v), total(v * v)


def sums_third(v, b_ref, u0_ref, coef):
    b, u0 = unpacked(b_ref), u0_ref[...]
    r1 = b - coef[:, 0:1] * u0
    d1 = r1 + coef[:, 1:2] * b
    return total(d1 * v), total(v * v), total(r1 * v), total(r1 * r1)


def gather_plane(array):
    return round_of(jnp.concatenate(round_of(array, "y"), axis=1), "x")


def added(refs):
    got = (refs[0][...] + refs[1][...]) + (refs[2][...] + refs[3][...])
    return got[:, :WIDTH], got[:, WIDTH:]


def first_kernel(m0, m1, m2, m3, b_ref, u_ref, sums_ref):
    got, sums_ref[...] = added((m0, m1, m2, m3))
    u_ref[...] = got + SHRINKAGE * b_ref[...]


def second_kernel(m0, m1, m2, m3, b_ref, u0_ref, sums_ref, u1_ref, r1_ref, d1_ref, ar1_ref, coef_ref):
    got, sums = added((m0, m1, m2, m3))
    b, u0 = b_ref[...], u0_ref[...]
    y = got + SHRINKAGE * u0
    rr0, c0, q0 = sums_ref[:, 0:1], sums[:, 0:1], sums[:, 1:2]
    a0 = rr0 / c0
    rr1 = rr0 - 2.0 * a0 * c0 + a0 * a0 * q0
    b0 = rr1 / rr0
    r1 = b - a0 * u0
    ar1 = u0 - a0 * y
    r1_ref[...] = r1
    d1_ref[...] = r1 + b0 * b
    ar1_ref[...] = ar1
    u1_ref[...] = ar1 + b0 * u0
    coef_ref[...] = in_lanes(a0, b0)


def third_kernel(
    m0, m1, m2, m3, b_ref, u1_ref, r1_ref, d1_ref, ar1_ref, coef_ref, x2_ref, r2_ref, d2_ref, u2_ref, sums_ref
):
    got, sums = added((m0, m1, m2, m3))
    u1, d1, r1 = u1_ref[...], d1_ref[...], r1_ref[...]
    y = got + SHRINKAGE * u1
    c1, q1, p1, rr1 = (sums[:, k : k + 1] for k in range(4))
    a1 = rr1 / c1
    rr2 = rr1 - 2.0 * a1 * p1 + a1 * a1 * q1
    b1 = rr2 / rr1
    r2 = r1 - a1 * u1
    d2 = r2 + b1 * d1
    u2 = (ar1_ref[...] - a1 * y) + b1 * u1
    x2_ref[...] = coef_ref[:, 0:1] * b_ref[...] + a1 * d1
    r2_ref[...] = r2
    d2_ref[...] = d2
    u2_ref[...] = u2
    tile = jnp.concatenate([in_lanes(total(d2 * u2), total(r2 * r2)), jnp.zeros((LANES - SIDES, LANES), F32)], axis=0)
    sums_ref[...] = jnp.transpose(tile)[0:8, :]


def last_kernel(sums_ref, x2_ref, r2_ref, d2_ref, u2_ref, at_ref, x_ref, r_ref, s_ref):
    got = jnp.transpose(jnp.sum(sums_ref[...], axis=0))[0:SIDES, :]
    a2 = got[:, 1:2] / got[:, 0:1]
    x = x2_ref[...] + a2 * d2_ref[...]
    r = r2_ref[...] - a2 * u2_ref[...]
    x_ref[...] = x
    r_ref[...] = r
    place = lax.broadcasted_iota(jnp.int32, (WIDTH, LANES), 0)
    pick = jnp.where(place == at_ref[...], 1.0, 0.0).astype(BF16)
    parts = [jnp.dot(p, pick, preferred_element_type=F32) for p in split3(r + SHRINKAGE * x)]
    s_ref[...] = jnp.abs((parts[0] + parts[1]) + parts[2])


def body(points, targets, cal_offset):
    small = 4 * 2**20
    vector = f32(SIDES, WIDTH)
    tile = f32(SIDES, LANES)
    b = targets
    scratch = [pltpu.VMEM((SIDES, WIDTH), F32), pltpu.SemaphoreType.DMA((2,))]
    outs = [jax.ShapeDtypeStruct((160, WIDTH), BF16)]
    in_hbm = [pltpu.with_memory_space_constraint(array, pltpu.HBM) for array in (points, b)]
    pack = call(pack_kernel, outs, small, scratch, in_specs=[HB, HB], name="pack")(*in_hbm)[0]
    bj = gather_plane(pack)
    pair = jnp.concatenate([pack[0:64], swap(points, "c", 1, 2)], axis=1)
    pairs = [pair] + [swap(pair, Z, m) for m in (1, 2, 3)]
    xi = jnp.concatenate([p[:, :WIDTH] for p in pairs] + [p[:, WIDTH:] for p in pairs], axis=1)
    prepare = functools.partial(prepare_kernel, 3.0 / points.shape[0])
    right = call(prepare, [jax.ShapeDtypeStruct((256, xi.shape[1]), BF16)], small, name="prepare")(xi)[0]
    msgs, blocks = first_product(bj, right)
    u0, sums = call(first_kernel, [vector, tile], small, name="first")(*msgs, b)
    u0j = gather_plane(u0)
    msgs = product(sums_second, u0j, [bj], blocks)
    u1, r1, d1, ar1, coef = call(second_kernel, [vector] * 4 + [tile], small, name="second")(*msgs, b, u0, sums)
    msgs = product(sums_third, gather_plane(u1), [bj, u0j], blocks, (coef,))
    x2, r2, d2, u2, part = call(third_kernel, [vector] * 4 + [f32(8, LANES)], small, name="third")(
        *msgs, b, u1, r1, d1, ar1, coef
    )
    part = part + swap(part, "c", 1, 2)
    parts = lax.all_to_all(
        jnp.broadcast_to(part[None], (64, 8, LANES)), ("x", "y", *Z), split_axis=0, concat_axis=0, tiled=True
    )
    return tuple(
        call(last_kernel, [vector, vector, tile], small, name="last")(
            parts, x2, r2, d2, u2, cal_offset.reshape(1, LANES)
        )
    )


def solution(mesh):
    grid = Mesh(mesh.devices.reshape(4, 4, 2, 2, 2), ALL)
    return jax.shard_map(
        body,
        mesh=grid,
        in_specs=(P(None, ALL), P(None, ALL), P(ALL)),
        out_specs=(P(None, ALL), P(None, ALL), P(None, ALL)),
        check_vma=False,
    )
```

```python
import functools

import jax
import jax.numpy as jnp
from jax import lax
from jax.experimental import pallas as pl
from jax.experimental.pallas import tpu as pltpu
from jax.sharding import Mesh, PartitionSpec as P

ALL = ("x", "y", "zl", "c", "zh")
Z = ("zl", "zh")
BF16, F32, F8 = jnp.bfloat16, jnp.float32, jnp.float8_e4m3fn
SHRINKAGE = 0.5
LOG2E = 1.4426950408889634
VM = pl.BlockSpec(memory_space=pltpu.VMEM)
HB = pl.BlockSpec(memory_space=pltpu.HBM)
TILE, ROWS, DEPTH = 512, 64, 4
NEAR, KEEP = (1, 1, 1, 4), 2
FORM_ROOM, APPLY_ROOM = 3 * 2**20, 1 * 2**20
SIDES, WIDTH, LANES = 32, 384, 128


def call(kernel, outs, limit, scratch=(), cost=None, in_specs=None, out_specs=None, name=None):
    if cost is not None:
        cost = pl.CostEstimate(flops=0, transcendentals=0, bytes_accessed=int(cost * 3.6e6))
    return lambda *args: pl.pallas_call(
        kernel,
        out_shape=outs,
        in_specs=in_specs or [VM] * len(args),
        out_specs=out_specs or [VM] * len(outs),
        scratch_shapes=scratch,
        compiler_params=pltpu.CompilerParams(vmem_limit_bytes=limit),
        cost_estimate=cost,
        name=name,
    )(*args)


def f32(*shape):
    return jax.ShapeDtypeStruct(shape, F32)


def swap(array, axis, k, size=4):
    return lax.ppermute(array, axis, [(i, i ^ k) for i in range(size)])


def round_of(array, axis):
    return [array] + [swap(array, axis, k) for k in (1, 3, 2)]


def split3(a):
    first = a.astype(BF16)
    rest = a - first.astype(F32)
    second = rest.astype(BF16)
    return first, second, (rest - second.astype(F32)).astype(BF16)


def tail_rows(first, second, n):
    rows = [part.astype(F32) for part in (*first, *second)]
    return jnp.concatenate([*rows, jnp.zeros((10, n), F32)], axis=0).astype(BF16)


def pack_kernel(points_ref, targets_ref, out_ref, targets, sems):
    copies = [
        pltpu.make_async_copy(points_ref, out_ref.at[0:64, :], sems.at[0]),
        pltpu.make_async_copy(targets_ref, targets, sems.at[1]),
    ]
    for copy in copies:
        copy.start()
    copies[1].wait()
    for place, part in enumerate(split3(targets[...])):
        out_ref[64 + place * SIDES : 64 + place * SIDES + SIDES, :] = part
    copies[0].wait()


def unpacked(ref):
    parts = [ref[64 + place * SIDES : 64 + place * SIDES + SIDES, :].astype(F32) for place in range(3)]
    return (parts[0] + parts[1]) + parts[2]


def prepare_kernel(sharpness, xi_ref, right):
    columns = xi_ref.shape[1]
    xi = xi_ref[...].astype(F32)
    sq = jnp.sum(xi * xi, axis=0, keepdims=True) * (-sharpness * LOG2E)
    for place, part in enumerate(split3(xi * (2.0 * sharpness * LOG2E))):
        right[place * 64 : place * 64 + 64, :] = part
    ones = [jnp.ones((1, columns), F32)] * 3
    right[192:208, :] = tail_rows(split3(sq), ones, columns)
    right[208:256, :] = jnp.zeros((48, columns), BF16)


def form_kernel(sharpness, kind, near, *refs):
    pack_ref, right, *refs = refs
    acc_ref, refs = (None, refs) if kind == "first" else (refs[0], refs[1:])
    tiles = right.shape[1] // TILE
    hi_refs, refs = refs[:tiles], refs[tiles:]
    near_refs, refs = refs[:near], refs[near:]
    far_ref, refs = (refs[0], refs[1:]) if near < tiles else (None, refs)
    out_ref, left_t, left, *own = refs
    if far_ref is not None:
        stage, sems = own
    count = pack_ref.shape[1]
    xj = pack_ref[0:64, :]
    xf = xj.astype(F32)
    sq = jnp.sum(xf * xf, axis=0, keepdims=True) * (-sharpness * LOG2E)
    for place in range(3):
        left_t[place * 64 : place * 64 + 64, :] = xj
    ones = [jnp.ones((1, count), F32)] * 3
    left_t[192:208, :] = tail_rows(ones, split3(sq), count)
    left_t[208:256, :] = jnp.zeros((48, count), BF16)
    for r in range(count // 128):
        at = slice(r * 128, r * 128 + 128)
        left[at, :] = left_t[:, at].T
    finish_tile(kind, sums_first, unpacked(pack_ref), (), acc_ref, None, out_ref)

    def copy(c, slot):
        return pltpu.make_async_copy(stage.at[slot], far_ref.at[c - near], sems.at[slot])

    def step(units, c, slot):
        starts = [pl.multiple_of(c * TILE + m * 256, 256) for m in range(2)]
        lows = near_refs[c] if slot is None else stage.at[slot]

        def finish(at, m, value):
            value = jnp.exp2(value)
            high = value.astype(BF16)
            hi_refs[c][at, m * 256 : m * 256 + 256] = high
            lows[at, m * 256 : m * 256 + 256] = (value - high.astype(F32)).astype(BF16)

        for m in range(2):
            pltpu.matmul_push_rhs(right[:, pl.ds(starts[m], 256)], 0, m)
        waiting = []
        for r in range(count // ROWS):
            at = slice(r * ROWS, r * ROWS + ROWS)
            for m in range(2):
                unit = units[m][r % DEPTH]
                pltpu.matmul_acc_lhs(unit, left[at, :], load_staged_rhs=0 if r == 0 else None)
                waiting.append((at, m, unit))
            if len(waiting) > 2 * (DEPTH - 1):
                for _ in range(2):
                    at, m, unit = waiting.pop(0)
                    finish(at, m, pltpu.matmul_pop(unit))
        for at, m, unit in waiting:
            finish(at, m, pltpu.matmul_pop(unit))
        turn = 0
        for k in range(count // 256):
            rows = slice(k * 256, k * 256 + 256)
            for source, which, height in ((hi_refs[c], -2, 96), (lows, -1, 64)):
                for m in range(2):
                    pltpu.matmul_push_rhs(source[rows, m * 256 : m * 256 + 256], turn % 2, m)
                for m in range(2):
                    pltpu.matmul_acc_lhs(units[m][which], pack_ref[64 : 64 + height, rows], load_staged_rhs=turn % 2)
                turn += 1
        for m in range(2):
            a, b = pltpu.matmul_pop(units[m][-2]), pltpu.matmul_pop(units[m][-1])
            value = a[0:SIDES] + (a[SIDES : 2 * SIDES] + ((b[0:SIDES] + b[SIDES:]) + a[2 * SIDES :]))
            if acc_ref is not None:
                value = value + acc_ref[:, pl.ds(starts[m], 256)]
            out_ref[:, pl.ds(starts[m], 256)] = value

    def steps(*units):
        each = len(units) // 2
        units = (units[:each], units[each:])
        for c in range(near, tiles):
            slot = (c - near) % KEEP
            if c >= near + KEEP:
                copy(c - KEEP, slot).wait()
            step(units, c, slot)
            copy(c, slot).start()
        for c in range(near):
            step(units, c, None)
        for c in range(max(near, tiles - KEEP), tiles):
            copy(c, (c - near) % KEEP).wait()

    heights = [ROWS] * DEPTH + [96, 64]
    pl.run_scoped(steps, *[pltpu.ACC(m)((h, 256), F32) for m in range(2) for h in heights])


def finish_tile(kind, sums, v, extra, acc_ref, tile_ref, out_ref):
    width = out_ref.shape[1] - LANES
    if kind == "own":
        tile = tile_ref[:, tile_ref.shape[1] - LANES :]
    else:
        tile = in_lanes(*sums(v, *extra))
        if acc_ref is not None:
            tile = tile + acc_ref[:, acc_ref.shape[1] - LANES :]
    out_ref[:, width:] = tile


def form(kind, near, pack, right, acc):
    count, width = pack.shape[1], right.shape[1]
    tiles = width // TILE
    outs = [pltpu.VMEM((count, TILE), BF16)] * (tiles + near)
    specs = [VM] * (tiles + near)
    scratch = [pltpu.VMEM((256, count), BF16), pltpu.VMEM((count, 256), BF16)]
    keep = min(KEEP, tiles - near)
    if keep:
        outs.append(pltpu.HBM((tiles - near, count, TILE), BF16))
        specs.append(HB)
        scratch += [pltpu.VMEM((keep, count, TILE), BF16), pltpu.SemaphoreType.DMA((keep,))]
    *parts, out = call(
        functools.partial(form_kernel, 3.0 / 64, kind, near),
        outs + [f32(SIDES, width + LANES)],
        FORM_ROOM + 3 * 2**19 * keep,
        scratch,
        cost=8.5,
        out_specs=specs + [VM],
        name="form",
    )(pack, right, *acc)
    return (parts[:tiles], parts[tiles : tiles + near], parts[tiles + near :]), out


def apply_kernel(sums, kind, columns, n_extra, all_tiles, near, *refs):
    v_ref, *refs = refs
    extra, refs = refs[:n_extra], refs[n_extra:]
    hi_refs, refs = refs[:all_tiles], refs[all_tiles:]
    near_refs, refs = refs[:near], refs[near:]
    far_ref, refs = (refs[0], refs[1:]) if near < all_tiles else (None, refs)
    acc_ref, refs = (None, refs) if kind == "first" else (refs[0], refs[1:])
    tile_ref, refs = (refs[0], refs[1:]) if kind == "own" else (None, refs)
    out_ref, parts, *own = refs
    if own:
        slots, sems = own
    tiles = range(columns // TILE, (columns + out_ref.shape[1] - LANES) // TILE)
    far_tiles = [c for c in tiles if c >= near]

    def copy(c):
        slot = c - far_tiles[0]
        return pltpu.make_async_copy(far_ref.at[c - near], slots.at[slot], sems.at[slot])

    for c in far_tiles:
        copy(c).start()
    v = v_ref[...]
    for place, part in enumerate(split3(v)):
        parts[place * SIDES : place * SIDES + SIDES, :] = part
    for c in tiles:
        cols, from_cols = (slice(at, at + TILE) for at in (c * TILE - columns, c * TILE))
        a = jnp.dot(parts[...], hi_refs[c][...], preferred_element_type=F32)
        value = a[0:SIDES] + (a[SIDES : 2 * SIDES] + a[2 * SIDES :])
        if acc_ref is not None:
            value = value + acc_ref[:, from_cols]
        out_ref[:, cols] = value
    finish_tile(kind, sums, v, extra, acc_ref, tile_ref, out_ref)
    for c in tiles:
        cols, from_cols = (slice(at, at + TILE) for at in (c * TILE - columns, c * TILE))
        if c >= near:
            copy(c).wait()
            low = slots[c - far_tiles[0]]
        else:
            low = near_refs[c][...]
        b = jnp.dot(parts[0 : 2 * SIDES, :], low, preferred_element_type=F32)
        out_ref[:, cols] = out_ref[:, cols] + (b[0:SIDES] + b[SIDES:])


def apply_block(sums, kind, columns, width, v, extra, hi, near, far, acc, tile):
    count = hi[0].shape[0]
    slots = sum(c >= len(near) for c in range(columns // TILE, (columns + width) // TILE))
    scratch = [pltpu.VMEM((3 * SIDES, count), BF16)]
    if slots:
        scratch += [pltpu.VMEM((slots, count, TILE), BF16), pltpu.SemaphoreType.DMA((slots,))]
    args, specs = [v, *extra, *hi], [VM] * (1 + len(extra) + len(hi))
    args += [*near, *[pltpu.with_memory_space_constraint(array, pltpu.HBM) for array in far]]
    specs += [VM] * len(near) + [HB] * len(far)
    return call(
        functools.partial(apply_kernel, sums, kind, columns, len(extra), len(hi), len(near)),
        [f32(SIDES, width + LANES)],
        APPLY_ROOM + 3 * 2**19 * slots,
        scratch,
        cost=(4.4 if slots else 3.2) * width / 3072,
        in_specs=specs + [VM] * len(acc + tile),
        name="apply",
    )(*args, *acc, *tile)[0]


def summed(own, other):
    fold = call(fold_kernel, [f32(SIDES, WIDTH + LANES)] * 4, 2**20, name="fold")
    parts = fold(own, swap(other, "c", 1, 2))
    return [parts[0]] + [swap(parts[m], Z, m) for m in (1, 3, 2)]


def first_product(packs, right):
    blocks, acc = [], []
    for k, pack in enumerate(packs):
        block, out = form("next" if k else "first", NEAR[k], pack, right, acc)
        blocks.append(block)
        acc = [out]
    half = 4 * WIDTH
    halves = [jnp.concatenate([out[:, at : at + half], out[:, 2 * half :]], axis=1) for at in (0, half)]
    return summed(*halves), blocks


def product(sums, vectors, extras, blocks, common=()):
    half, last = 4 * WIDTH, len(vectors) - 1

    def work(kind, k, columns, width, acc, tile):
        extra = [e[k] for e in extras] + list(common)
        return apply_block(sums, kind, columns, width, vectors[k], extra, *blocks[k], acc, tile)

    acc = []
    for k in range(last):
        acc = [work("next" if k else "first", k, 0, 2 * half, acc, [])]
    other = work("other", last, half, half, acc, [])
    return summed(work("own", last, 0, half, acc, [other]), other)


def fold_kernel(own_ref, got_ref, *outs):
    value = own_ref[...] + got_ref[...]
    for m, out in enumerate(outs):
        out[:, :WIDTH] = value[:, m * WIDTH : m * WIDTH + WIDTH]
        out[:, WIDTH:] = value[:, 4 * WIDTH :]


def total(a):
    return jnp.sum(a, axis=1, keepdims=True)


def in_lanes(*values):
    lane = lax.broadcasted_iota(jnp.int32, (SIDES, LANES), 1)
    tile = jnp.zeros((SIDES, LANES), F32)
    for place, value in enumerate(values):
        tile = jnp.where(lane == place, value, tile)
    return tile


def sums_first(v):
    return (total(v * v),)


def sums_second(v, b_ref):
    return total(unpacked(b_ref) * v), total(v * v)


def sums_third(v, b_ref, u0_ref, coef):
    b, u0 = unpacked(b_ref), u0_ref[...]
    r1 = b - coef[:, 0:1] * u0
    d1 = r1 + coef[:, 1:2] * b
    return total(d1 * v), total(v * v), total(r1 * v), total(r1 * r1)


def gather_plane(array):
    return round_of(jnp.concatenate(round_of(array, "y"), axis=1), "x")


def added(refs):
    got = (refs[0][...] + refs[1][...]) + (refs[2][...] + refs[3][...])
    return got[:, :WIDTH], got[:, WIDTH:]


def first_kernel(m0, m1, m2, m3, b_ref, u_ref, sums_ref):
    got, sums_ref[...] = added((m0, m1, m2, m3))
    u_ref[...] = got + SHRINKAGE * b_ref[...]


def second_kernel(m0, m1, m2, m3, b_ref, u0_ref, sums_ref, u1_ref, r1_ref, d1_ref, ar1_ref, coef_ref):
    got, sums = added((m0, m1, m2, m3))
    b, u0 = b_ref[...], u0_ref[...]
    y = got + SHRINKAGE * u0
    rr0, c0, q0 = sums_ref[:, 0:1], sums[:, 0:1], sums[:, 1:2]
    a0 = rr0 / c0
    rr1 = rr0 - 2.0 * a0 * c0 + a0 * a0 * q0
    b0 = rr1 / rr0
    r1 = b - a0 * u0
    ar1 = u0 - a0 * y
    r1_ref[...] = r1
    d1_ref[...] = r1 + b0 * b
    ar1_ref[...] = ar1
    u1_ref[...] = ar1 + b0 * u0
    coef_ref[...] = in_lanes(a0, b0)


def third_kernel(
    m0, m1, m2, m3, b_ref, u1_ref, r1_ref, d1_ref, ar1_ref, coef_ref, x2_ref, r2_ref, d2_ref, u2_ref, sums_ref
):
    got, sums = added((m0, m1, m2, m3))
    u1, d1, r1 = u1_ref[...], d1_ref[...], r1_ref[...]
    y = got + SHRINKAGE * u1
    c1, q1, p1, rr1 = (sums[:, k : k + 1] for k in range(4))
    a1 = rr1 / c1
    rr2 = rr1 - 2.0 * a1 * p1 + a1 * a1 * q1
    b1 = rr2 / rr1
    r2 = r1 - a1 * u1
    d2 = r2 + b1 * d1
    u2 = (ar1_ref[...] - a1 * y) + b1 * u1
    x2_ref[...] = coef_ref[:, 0:1] * b_ref[...] + a1 * d1
    r2_ref[...] = r2
    d2_ref[...] = d2
    u2_ref[...] = u2
    tile = jnp.concatenate([in_lanes(total(d2 * u2), total(r2 * r2)), jnp.zeros((LANES - SIDES, LANES), F32)], axis=0)
    sums_ref[...] = jnp.transpose(tile)[0:8, :]


def last_kernel(sums_ref, x2_ref, r2_ref, d2_ref, u2_ref, at_ref, x_ref, r_ref, s_ref):
    got = jnp.transpose(jnp.sum(sums_ref[...], axis=0))[0:SIDES, :]
    a2 = got[:, 1:2] / got[:, 0:1]
    x = x2_ref[...] + a2 * d2_ref[...]
    r = r2_ref[...] - a2 * u2_ref[...]
    x_ref[...] = x
    r_ref[...] = r
    place = lax.broadcasted_iota(jnp.int32, (WIDTH, LANES), 0)
    pick = jnp.where(place == at_ref[...], 1.0, 0.0).astype(BF16)
    parts = [jnp.dot(p, pick, preferred_element_type=F32) for p in split3(r + SHRINKAGE * x)]
    s_ref[...] = jnp.abs((parts[0] + parts[1]) + parts[2])


def body(points, targets, cal_offset):
    small = 4 * 2**20
    vector = f32(SIDES, WIDTH)
    tile = f32(SIDES, LANES)
    b = targets
    scratch = [pltpu.VMEM((SIDES, WIDTH), F32), pltpu.SemaphoreType.DMA((2,))]
    outs = [jax.ShapeDtypeStruct((160, WIDTH), BF16)]
    in_hbm = [pltpu.with_memory_space_constraint(array, pltpu.HBM) for array in (points, b)]
    pack = call(pack_kernel, outs, small, scratch, in_specs=[HB, HB], name="pack")(*in_hbm)[0]
    bj = gather_plane(pack)
    pair = jnp.concatenate([pack[0:64], swap(points, "c", 1, 2)], axis=1)
    pairs = [pair] + [swap(pair, Z, m) for m in (1, 2, 3)]
    xi = jnp.concatenate([p[:, :WIDTH] for p in pairs] + [p[:, WIDTH:] for p in pairs], axis=1)
    prepare = functools.partial(prepare_kernel, 3.0 / points.shape[0])
    right = call(prepare, [jax.ShapeDtypeStruct((256, xi.shape[1]), BF16)], small, name="prepare")(xi)[0]
    msgs, blocks = first_product(bj, right)
    u0, sums = call(first_kernel, [vector, tile], small, name="first")(*msgs, b)
    u0j = gather_plane(u0)
    msgs = product(sums_second, u0j, [bj], blocks)
    u1, r1, d1, ar1, coef = call(second_kernel, [vector] * 4 + [tile], small, name="second")(*msgs, b, u0, sums)
    msgs = product(sums_third, gather_plane(u1), [bj, u0j], blocks, (coef,))
    x2, r2, d2, u2, part = call(third_kernel, [vector] * 4 + [f32(8, LANES)], small, name="third")(
        *msgs, b, u1, r1, d1, ar1, coef
    )
    part = part + swap(part, "c", 1, 2)
    parts = lax.all_to_all(
        jnp.broadcast_to(part[None], (64, 8, LANES)), ("x", "y", *Z), split_axis=0, concat_axis=0, tiled=True
    )
    return tuple(
        call(last_kernel, [vector, vector, tile], small, name="last")(
            parts, x2, r2, d2, u2, cal_offset.reshape(1, LANES)
        )
    )


def solution(mesh):
    grid = Mesh(mesh.devices.reshape(4, 4, 2, 2, 2), ALL)
    return jax.shard_map(
        body,
        mesh=grid,
        in_specs=(P(None, ALL), P(None, ALL), P(ALL)),
        out_specs=(P(None, ALL), P(None, ALL), P(None, ALL)),
        check_vma=False,
    )
```

```python
import functools

import jax
import jax.numpy as jnp
from jax import lax
from jax.experimental import pallas as pl
from jax.experimental.pallas import tpu as pltpu
from jax.sharding import Mesh, PartitionSpec as P

ALL = ("x", "y", "zl", "c", "zh")
Z = ("zl", "zh")
BF16, F32, F8 = jnp.bfloat16, jnp.float32, jnp.float8_e4m3fn
SHRINKAGE = 0.5
LOG2E = 1.4426950408889634
VM = pl.BlockSpec(memory_space=pltpu.VMEM)
HB = pl.BlockSpec(memory_space=pltpu.HBM)
TILE, ROWS, DEPTH = 512, 64, 4
NEAR, KEEP = (1, 1, 1, 4), 2
FORM_ROOM, APPLY_ROOM = 3 * 2**20, 1 * 2**20
SIDES, WIDTH, LANES = 32, 384, 128


def call(kernel, outs, limit, scratch=(), cost=None, in_specs=None, out_specs=None, name=None):
    if cost is not None:
        cost = pl.CostEstimate(flops=0, transcendentals=0, bytes_accessed=int(cost * 3.6e6))
    return lambda *args: pl.pallas_call(
        kernel,
        out_shape=outs,
        in_specs=in_specs or [VM] * len(args),
        out_specs=out_specs or [VM] * len(outs),
        scratch_shapes=scratch,
        compiler_params=pltpu.CompilerParams(vmem_limit_bytes=limit),
        cost_estimate=cost,
        name=name,
    )(*args)


def f32(*shape):
    return jax.ShapeDtypeStruct(shape, F32)


def swap(array, axis, k, size=4):
    return lax.ppermute(array, axis, [(i, i ^ k) for i in range(size)])


def round_of(array, axis):
    return [array] + [swap(array, axis, k) for k in (1, 3, 2)]


def split3(a):
    first = a.astype(BF16)
    rest = a - first.astype(F32)
    second = rest.astype(BF16)
    return first, second, (rest - second.astype(F32)).astype(BF16)


def tail_rows(first, second, n):
    rows = [part.astype(F32) for part in (*first, *second)]
    return jnp.concatenate([*rows, jnp.zeros((10, n), F32)], axis=0).astype(BF16)


def pack_kernel(points_ref, targets_ref, out_ref, targets, sems):
    copies = [
        pltpu.make_async_copy(points_ref, out_ref.at[0:64, :], sems.at[0]),
        pltpu.make_async_copy(targets_ref, targets, sems.at[1]),
    ]
    for copy in copies:
        copy.start()
    copies[1].wait()
    for place, part in enumerate(split3(targets[...])):
        out_ref[64 + place * SIDES : 64 + place * SIDES + SIDES, :] = part
    copies[0].wait()


def unpacked(ref):
    parts = [ref[64 + place * SIDES : 64 + place * SIDES + SIDES, :].astype(F32) for place in range(3)]
    return (parts[0] + parts[1]) + parts[2]


def prepare_kernel(sharpness, xi_ref, right):
    columns = xi_ref.shape[1]
    xi = xi_ref[...].astype(F32)
    sq = jnp.sum(xi * xi, axis=0, keepdims=True) * (-sharpness * LOG2E)
    for place, part in enumerate(split3(xi * (2.0 * sharpness * LOG2E))):
        right[place * 64 : place * 64 + 64, :] = part
    ones = [jnp.ones((1, columns), F32)] * 3
    right[192:208, :] = tail_rows(split3(sq), ones, columns)
    right[208:256, :] = jnp.zeros((48, columns), BF16)


def form_kernel(sharpness, kind, near, *refs):
    pack_ref, right, *refs = refs
    acc_ref, refs = (None, refs) if kind == "first" else (refs[0], refs[1:])
    tiles = right.shape[1] // TILE
    hi_refs, refs = refs[:tiles], refs[tiles:]
    near_refs, refs = refs[:near], refs[near:]
    far_ref, refs = (refs[0], refs[1:]) if near < tiles else (None, refs)
    out_ref, left_t, left, *own = refs
    if far_ref is not None:
        stage, sems = own
    count = pack_ref.shape[1]
    xj = pack_ref[0:64, :]
    xf = xj.astype(F32)
    sq = jnp.sum(xf * xf, axis=0, keepdims=True) * (-sharpness * LOG2E)
    for place in range(3):
        left_t[place * 64 : place * 64 + 64, :] = xj
    ones = [jnp.ones((1, count), F32)] * 3
    left_t[192:208, :] = tail_rows(ones, split3(sq), count)
    left_t[208:256, :] = jnp.zeros((48, count), BF16)
    for r in range(count // 128):
        at = slice(r * 128, r * 128 + 128)
        left[at, :] = left_t[:, at].T
    finish_tile(kind, sums_first, unpacked(pack_ref), (), acc_ref, None, out_ref)

    def copy(c, slot):
        return pltpu.make_async_copy(stage.at[slot], far_ref.at[c - near], sems.at[slot])

    def step(units, c, slot, earlier):
        starts = [pl.multiple_of(c * TILE + m * 256, 256) for m in range(2)]
        lows = near_refs[c] if slot is None else stage.at[slot]

        def finish(at, m, value):
            value = jnp.exp2(value)
            high = value.astype(BF16)
            hi_refs[c][at, m * 256 : m * 256 + 256] = high
            lows[at, m * 256 : m * 256 + 256] = (value - high.astype(F32)).astype(BF16)

        waiting = []
        groups, turn = 3, 0
        for r in range(count // ROWS):
            fresh = r % (count // ROWS // groups) == 0
            if fresh:
                if r and earlier is not None:
                    multiply(units, *earlier, turn)
                    turn += 1
                if r == 0 or earlier is not None:
                    for m in range(2):
                        pltpu.matmul_push_rhs(right[:, pl.ds(starts[m], 256)], 0, m)
            load = 0 if r == 0 or (fresh and earlier is not None) else None
            at = slice(r * ROWS, r * ROWS + ROWS)
            for m in range(2):
                unit = units[m][r % DEPTH]
                pltpu.matmul_acc_lhs(unit, left[at, :], load_staged_rhs=load)
                waiting.append((at, m, unit))
            if len(waiting) > 2 * (DEPTH - 1):
                for _ in range(2):
                    at, m, unit = waiting.pop(0)
                    finish(at, m, pltpu.matmul_pop(unit))
        if earlier is not None:
            multiply(units, *earlier, turn)
            store(units, earlier[0])
        for at, m, unit in waiting:
            finish(at, m, pltpu.matmul_pop(unit))
        return c, lows

    def multiply(units, c, lows, part):
        turn, each = 0, count // 256 // 3
        for k in range(part * each, part * each + each):
            rows = slice(k * 256, k * 256 + 256)
            for source, which, height in ((hi_refs[c], -2, 96), (lows, -1, 64)):
                for m in range(2):
                    pltpu.matmul_push_rhs(source[rows, m * 256 : m * 256 + 256], turn % 2, m)
                for m in range(2):
                    pltpu.matmul_acc_lhs(units[m][which], pack_ref[64 : 64 + height, rows], load_staged_rhs=turn % 2)
                turn += 1

    def store(units, c):
        for m in range(2):
            cols = slice(c * TILE + m * 256, c * TILE + m * 256 + 256)
            a, b = pltpu.matmul_pop(units[m][-2]), pltpu.matmul_pop(units[m][-1])
            value = a[0:SIDES] + (a[SIDES : 2 * SIDES] + ((b[0:SIDES] + b[SIDES:]) + a[2 * SIDES :]))
            if acc_ref is not None:
                value = value + acc_ref[:, cols]
            out_ref[:, cols] = value

    def steps(*units):
        each = len(units) // 2
        units = (units[:each], units[each:])
        earlier = None
        for c in range(near, tiles):
            slot = (c - near) % KEEP
            if c >= near + KEEP:
                copy(c - KEEP, slot).wait()
            earlier = step(units, c, slot, earlier)
            copy(c, slot).start()
        for c in range(near):
            earlier = step(units, c, None, earlier)
        for part in range(3):
            multiply(units, *earlier, part)
        store(units, earlier[0])
        for c in range(max(near, tiles - KEEP), tiles):
            copy(c, (c - near) % KEEP).wait()

    heights = [ROWS] * DEPTH + [96, 64]
    pl.run_scoped(steps, *[pltpu.ACC(m)((h, 256), F32) for m in range(2) for h in heights])


def finish_tile(kind, sums, v, extra, acc_ref, tile_ref, out_ref):
    width = out_ref.shape[1] - LANES
    if kind == "own":
        tile = tile_ref[:, tile_ref.shape[1] - LANES :]
    else:
        tile = in_lanes(*sums(v, *extra))
        if acc_ref is not None:
            tile = tile + acc_ref[:, acc_ref.shape[1] - LANES :]
    out_ref[:, width:] = tile


def form(kind, near, pack, right, acc):
    count, width = pack.shape[1], right.shape[1]
    tiles = width // TILE
    outs = [pltpu.VMEM((count, TILE), BF16)] * (tiles + near)
    specs = [VM] * (tiles + near)
    scratch = [pltpu.VMEM((256, count), BF16), pltpu.VMEM((count, 256), BF16)]
    keep = min(KEEP, tiles - near)
    if keep:
        outs.append(pltpu.HBM((tiles - near, count, TILE), BF16))
        specs.append(HB)
        scratch += [pltpu.VMEM((keep, count, TILE), BF16), pltpu.SemaphoreType.DMA((keep,))]
    *parts, out = call(
        functools.partial(form_kernel, 3.0 / 64, kind, near),
        outs + [f32(SIDES, width + LANES)],
        FORM_ROOM + 3 * 2**19 * keep,
        scratch,
        cost=8.5,
        out_specs=specs + [VM],
        name="form",
    )(pack, right, *acc)
    return (parts[:tiles], parts[tiles : tiles + near], parts[tiles + near :]), out


def apply_kernel(sums, kind, columns, n_extra, all_tiles, near, *refs):
    v_ref, *refs = refs
    extra, refs = refs[:n_extra], refs[n_extra:]
    hi_refs, refs = refs[:all_tiles], refs[all_tiles:]
    near_refs, refs = refs[:near], refs[near:]
    far_ref, refs = (refs[0], refs[1:]) if near < all_tiles else (None, refs)
    acc_ref, refs = (None, refs) if kind == "first" else (refs[0], refs[1:])
    tile_ref, refs = (refs[0], refs[1:]) if kind == "own" else (None, refs)
    out_ref, parts, *own = refs
    if own:
        slots, sems = own
    tiles = range(columns // TILE, (columns + out_ref.shape[1] - LANES) // TILE)
    far_tiles = [c for c in tiles if c >= near]

    def copy(c):
        slot = c - far_tiles[0]
        return pltpu.make_async_copy(far_ref.at[c - near], slots.at[slot], sems.at[slot])

    for c in far_tiles:
        copy(c).start()
    v = v_ref[...]
    for place, part in enumerate(split3(v)):
        parts[place * SIDES : place * SIDES + SIDES, :] = part
    for c in tiles:
        cols, from_cols = (slice(at, at + TILE) for at in (c * TILE - columns, c * TILE))
        a = jnp.dot(parts[...], hi_refs[c][...], preferred_element_type=F32)
        value = a[0:SIDES] + (a[SIDES : 2 * SIDES] + a[2 * SIDES :])
        if acc_ref is not None:
            value = value + acc_ref[:, from_cols]
        out_ref[:, cols] = value
    finish_tile(kind, sums, v, extra, acc_ref, tile_ref, out_ref)
    for c in tiles:
        cols, from_cols = (slice(at, at + TILE) for at in (c * TILE - columns, c * TILE))
        if c >= near:
            copy(c).wait()
            low = slots[c - far_tiles[0]]
        else:
            low = near_refs[c][...]
        b = jnp.dot(parts[0 : 2 * SIDES, :], low, preferred_element_type=F32)
        out_ref[:, cols] = out_ref[:, cols] + (b[0:SIDES] + b[SIDES:])


def apply_block(sums, kind, columns, width, v, extra, hi, near, far, acc, tile):
    count = hi[0].shape[0]
    slots = sum(c >= len(near) for c in range(columns // TILE, (columns + width) // TILE))
    scratch = [pltpu.VMEM((3 * SIDES, count), BF16)]
    if slots:
        scratch += [pltpu.VMEM((slots, count, TILE), BF16), pltpu.SemaphoreType.DMA((slots,))]
    args, specs = [v, *extra, *hi], [VM] * (1 + len(extra) + len(hi))
    args += [*near, *[pltpu.with_memory_space_constraint(array, pltpu.HBM) for array in far]]
    specs += [VM] * len(near) + [HB] * len(far)
    return call(
        functools.partial(apply_kernel, sums, kind, columns, len(extra), len(hi), len(near)),
        [f32(SIDES, width + LANES)],
        APPLY_ROOM + 3 * 2**19 * slots,
        scratch,
        cost=(4.4 if slots else 3.2) * width / 3072,
        in_specs=specs + [VM] * len(acc + tile),
        name="apply",
    )(*args, *acc, *tile)[0]


def summed(own, other):
    fold = call(fold_kernel, [f32(SIDES, WIDTH + LANES)] * 4, 2**20, name="fold")
    parts = fold(own, swap(other, "c", 1, 2))
    return [parts[0]] + [swap(parts[m], Z, m) for m in (1, 3, 2)]


def first_product(packs, right):
    blocks, acc = [], []
    for k, pack in enumerate(packs):
        block, out = form("next" if k else "first", NEAR[k], pack, right, acc)
        blocks.append(block)
        acc = [out]
    half = 4 * WIDTH
    halves = [jnp.concatenate([out[:, at : at + half], out[:, 2 * half :]], axis=1) for at in (0, half)]
    return summed(*halves), blocks


def product(sums, vectors, extras, blocks, common=()):
    half, last = 4 * WIDTH, len(vectors) - 1

    def work(kind, k, columns, width, acc, tile):
        extra = [e[k] for e in extras] + list(common)
        return apply_block(sums, kind, columns, width, vectors[k], extra, *blocks[k], acc, tile)

    acc = []
    for k in range(last):
        acc = [work("next" if k else "first", k, 0, 2 * half, acc, [])]
    other = work("other", last, half, half, acc, [])
    return summed(work("own", last, 0, half, acc, [other]), other)


def fold_kernel(own_ref, got_ref, *outs):
    value = own_ref[...] + got_ref[...]
    for m, out in enumerate(outs):
        out[:, :WIDTH] = value[:, m * WIDTH : m * WIDTH + WIDTH]
        out[:, WIDTH:] = value[:, 4 * WIDTH :]


def total(a):
    return jnp.sum(a, axis=1, keepdims=True)


def in_lanes(*values):
    lane = lax.broadcasted_iota(jnp.int32, (SIDES, LANES), 1)
    tile = jnp.zeros((SIDES, LANES), F32)
    for place, value in enumerate(values):
        tile = jnp.where(lane == place, value, tile)
    return tile


def sums_first(v):
    return (total(v * v),)


def sums_second(v, b_ref):
    return total(unpacked(b_ref) * v), total(v * v)


def sums_third(v, b_ref, u0_ref, coef):
    b, u0 = unpacked(b_ref), u0_ref[...]
    r1 = b - coef[:, 0:1] * u0
    d1 = r1 + coef[:, 1:2] * b
    return total(d1 * v), total(v * v), total(r1 * v), total(r1 * r1)


def gather_plane(array):
    return round_of(jnp.concatenate(round_of(array, "y"), axis=1), "x")


def added(refs):
    got = (refs[0][...] + refs[1][...]) + (refs[2][...] + refs[3][...])
    return got[:, :WIDTH], got[:, WIDTH:]


def first_kernel(m0, m1, m2, m3, b_ref, u_ref, sums_ref):
    got, sums_ref[...] = added((m0, m1, m2, m3))
    u_ref[...] = got + SHRINKAGE * b_ref[...]


def second_kernel(m0, m1, m2, m3, b_ref, u0_ref, sums_ref, u1_ref, r1_ref, d1_ref, ar1_ref, coef_ref):
    got, sums = added((m0, m1, m2, m3))
    b, u0 = b_ref[...], u0_ref[...]
    y = got + SHRINKAGE * u0
    rr0, c0, q0 = sums_ref[:, 0:1], sums[:, 0:1], sums[:, 1:2]
    a0 = rr0 / c0
    rr1 = rr0 - 2.0 * a0 * c0 + a0 * a0 * q0
    b0 = rr1 / rr0
    r1 = b - a0 * u0
    ar1 = u0 - a0 * y
    r1_ref[...] = r1
    d1_ref[...] = r1 + b0 * b
    ar1_ref[...] = ar1
    u1_ref[...] = ar1 + b0 * u0
    coef_ref[...] = in_lanes(a0, b0)


def third_kernel(
    m0, m1, m2, m3, b_ref, u1_ref, r1_ref, d1_ref, ar1_ref, coef_ref, x2_ref, r2_ref, d2_ref, u2_ref, sums_ref
):
    got, sums = added((m0, m1, m2, m3))
    u1, d1, r1 = u1_ref[...], d1_ref[...], r1_ref[...]
    y = got + SHRINKAGE * u1
    c1, q1, p1, rr1 = (sums[:, k : k + 1] for k in range(4))
    a1 = rr1 / c1
    rr2 = rr1 - 2.0 * a1 * p1 + a1 * a1 * q1
    b1 = rr2 / rr1
    r2 = r1 - a1 * u1
    d2 = r2 + b1 * d1
    u2 = (ar1_ref[...] - a1 * y) + b1 * u1
    x2_ref[...] = coef_ref[:, 0:1] * b_ref[...] + a1 * d1
    r2_ref[...] = r2
    d2_ref[...] = d2
    u2_ref[...] = u2
    tile = jnp.concatenate([in_lanes(total(d2 * u2), total(r2 * r2)), jnp.zeros((LANES - SIDES, LANES), F32)], axis=0)
    sums_ref[...] = jnp.transpose(tile)[0:8, :]


def last_kernel(sums_ref, x2_ref, r2_ref, d2_ref, u2_ref, at_ref, x_ref, r_ref, s_ref):
    got = jnp.transpose(jnp.sum(sums_ref[...], axis=0))[0:SIDES, :]
    a2 = got[:, 1:2] / got[:, 0:1]
    x = x2_ref[...] + a2 * d2_ref[...]
    r = r2_ref[...] - a2 * u2_ref[...]
    x_ref[...] = x
    r_ref[...] = r
    place = lax.broadcasted_iota(jnp.int32, (WIDTH, LANES), 0)
    pick = jnp.where(place == at_ref[...], 1.0, 0.0).astype(BF16)
    parts = [jnp.dot(p, pick, preferred_element_type=F32) for p in split3(r + SHRINKAGE * x)]
    s_ref[...] = jnp.abs((parts[0] + parts[1]) + parts[2])


def body(points, targets, cal_offset):
    small = 4 * 2**20
    vector = f32(SIDES, WIDTH)
    tile = f32(SIDES, LANES)
    b = targets
    scratch = [pltpu.VMEM((SIDES, WIDTH), F32), pltpu.SemaphoreType.DMA((2,))]
    outs = [jax.ShapeDtypeStruct((160, WIDTH), BF16)]
    in_hbm = [pltpu.with_memory_space_constraint(array, pltpu.HBM) for array in (points, b)]
    pack = call(pack_kernel, outs, small, scratch, in_specs=[HB, HB], name="pack")(*in_hbm)[0]
    bj = gather_plane(pack)
    pair = jnp.concatenate([pack[0:64], swap(points, "c", 1, 2)], axis=1)
    pairs = [pair] + [swap(pair, Z, m) for m in (1, 2, 3)]
    xi = jnp.concatenate([p[:, :WIDTH] for p in pairs] + [p[:, WIDTH:] for p in pairs], axis=1)
    prepare = functools.partial(prepare_kernel, 3.0 / points.shape[0])
    right = call(prepare, [jax.ShapeDtypeStruct((256, xi.shape[1]), BF16)], small, name="prepare")(xi)[0]
    msgs, blocks = first_product(bj, right)
    u0, sums = call(first_kernel, [vector, tile], small, name="first")(*msgs, b)
    u0j = gather_plane(u0)
    msgs = product(sums_second, u0j, [bj], blocks)
    u1, r1, d1, ar1, coef = call(second_kernel, [vector] * 4 + [tile], small, name="second")(*msgs, b, u0, sums)
    msgs = product(sums_third, gather_plane(u1), [bj, u0j], blocks, (coef,))
    x2, r2, d2, u2, part = call(third_kernel, [vector] * 4 + [f32(8, LANES)], small, name="third")(
        *msgs, b, u1, r1, d1, ar1, coef
    )
    part = part + swap(part, "c", 1, 2)
    parts = lax.all_to_all(
        jnp.broadcast_to(part[None], (64, 8, LANES)), ("x", "y", *Z), split_axis=0, concat_axis=0, tiled=True
    )
    return tuple(
        call(last_kernel, [vector, vector, tile], small, name="last")(
            parts, x2, r2, d2, u2, cal_offset.reshape(1, LANES)
        )
    )


def solution(mesh):
    grid = Mesh(mesh.devices.reshape(4, 4, 2, 2, 2), ALL)
    return jax.shard_map(
        body,
        mesh=grid,
        in_specs=(P(None, ALL), P(None, ALL), P(ALL)),
        out_specs=(P(None, ALL), P(None, ALL), P(None, ALL)),
        check_vma=False,
    )
```

```python
import functools

import jax
import jax.numpy as jnp
from jax import lax
from jax.experimental import pallas as pl
from jax.experimental.pallas import tpu as pltpu
from jax.sharding import Mesh, PartitionSpec as P

ALL = ("x", "y", "zl", "c", "zh")
Z = ("zl", "zh")
BF16, F32, F8 = jnp.bfloat16, jnp.float32, jnp.float8_e4m3fn
SHRINKAGE = 0.5
LOG2E = 1.4426950408889634
VM = pl.BlockSpec(memory_space=pltpu.VMEM)
HB = pl.BlockSpec(memory_space=pltpu.HBM)
TILE, ROWS, DEPTH = 512, 64, 4
NEAR, KEEP = (1, 1, 1, 4), 2
FORM_ROOM, APPLY_ROOM = 3 * 2**20, 1 * 2**20
SIDES, WIDTH, LANES = 32, 384, 128


def call(kernel, outs, limit, scratch=(), cost=None, in_specs=None, out_specs=None, name=None):
    if cost is not None:
        cost = pl.CostEstimate(flops=0, transcendentals=0, bytes_accessed=int(cost * 3.6e6))
    return lambda *args: pl.pallas_call(
        kernel,
        out_shape=outs,
        in_specs=in_specs or [VM] * len(args),
        out_specs=out_specs or [VM] * len(outs),
        scratch_shapes=scratch,
        compiler_params=pltpu.CompilerParams(vmem_limit_bytes=limit),
        cost_estimate=cost,
        name=name,
    )(*args)


def f32(*shape):
    return jax.ShapeDtypeStruct(shape, F32)


def swap(array, axis, k, size=4):
    return lax.ppermute(array, axis, [(i, i ^ k) for i in range(size)])


def round_of(array, axis):
    return [array] + [swap(array, axis, k) for k in (1, 3, 2)]


def split3(a):
    first = a.astype(BF16)
    rest = a - first.astype(F32)
    second = rest.astype(BF16)
    return first, second, (rest - second.astype(F32)).astype(BF16)


def tail_rows(first, second, n):
    rows = [part.astype(F32) for part in (*first, *second)]
    return jnp.concatenate([*rows, jnp.zeros((10, n), F32)], axis=0).astype(BF16)


def pack_kernel(points_ref, targets_ref, out_ref, targets, sems):
    copies = [
        pltpu.make_async_copy(points_ref, out_ref.at[0:64, :], sems.at[0]),
        pltpu.make_async_copy(targets_ref, targets, sems.at[1]),
    ]
    for copy in copies:
        copy.start()
    copies[1].wait()
    for place, part in enumerate(split3(targets[...])):
        out_ref[64 + place * SIDES : 64 + place * SIDES + SIDES, :] = part
    copies[0].wait()


def unpacked(ref):
    parts = [ref[64 + place * SIDES : 64 + place * SIDES + SIDES, :].astype(F32) for place in range(3)]
    return (parts[0] + parts[1]) + parts[2]


def prepare_kernel(sharpness, xi_ref, right):
    columns = xi_ref.shape[1]
    xi = xi_ref[...].astype(F32)
    sq = jnp.sum(xi * xi, axis=0, keepdims=True) * (-sharpness * LOG2E)
    for place, part in enumerate(split3(xi * (2.0 * sharpness * LOG2E))):
        right[place * 64 : place * 64 + 64, :] = part
    ones = [jnp.ones((1, columns), F32)] * 3
    right[192:208, :] = tail_rows(split3(sq), ones, columns)
    right[208:256, :] = jnp.zeros((48, columns), BF16)


def form_kernel(sharpness, kind, near, *refs):
    pack_ref, right, *refs = refs
    acc_ref, refs = (None, refs) if kind == "first" else (refs[0], refs[1:])
    tiles = right.shape[1] // TILE
    hi_refs, refs = refs[:tiles], refs[tiles:]
    near_refs, refs = refs[:near], refs[near:]
    far_ref, refs = (refs[0], refs[1:]) if near < tiles else (None, refs)
    out_ref, left_t, left, *own = refs
    if far_ref is not None:
        stage, sems = own
    count = pack_ref.shape[1]
    xj = pack_ref[0:64, :]
    xf = xj.astype(F32)
    sq = jnp.sum(xf * xf, axis=0, keepdims=True) * (-sharpness * LOG2E)
    for place in range(3):
        left_t[place * 64 : place * 64 + 64, :] = xj
    ones = [jnp.ones((1, count), F32)] * 3
    left_t[192:208, :] = tail_rows(ones, split3(sq), count)
    left_t[208:256, :] = jnp.zeros((48, count), BF16)
    for r in range(count // 128):
        at = slice(r * 128, r * 128 + 128)
        left[at, :] = left_t[:, at].T
    finish_tile(kind, sums_first, unpacked(pack_ref), (), acc_ref, None, out_ref)

    def copy(c, slot):
        return pltpu.make_async_copy(stage.at[slot], far_ref.at[c - near], sems.at[slot])

    def step(units, c, slot, earlier):
        starts = [pl.multiple_of(c * TILE + m * 256, 256) for m in range(2)]
        lows = near_refs[c] if slot is None else stage.at[slot]

        def finish(at, m, value):
            value = jnp.exp2(value)
            high = value.astype(BF16)
            hi_refs[c][at, m * 256 : m * 256 + 256] = high
            lows[at, m * 256 : m * 256 + 256] = (value - high.astype(F32)).astype(BF16)

        waiting = []
        groups, turn = 3, 0
        for r in range(count // ROWS):
            fresh = r % (count // ROWS // groups) == 0
            if fresh:
                if r and earlier is not None:
                    multiply(units, *earlier, turn)
                    turn += 1
                if r == 0 or earlier is not None:
                    for m in range(2):
                        pltpu.matmul_push_rhs(right[:, pl.ds(starts[m], 256)], 0, m)
            load = 0 if r == 0 or (fresh and earlier is not None) else None
            at = slice(r * ROWS, r * ROWS + ROWS)
            for m in range(2):
                unit = units[m][r % DEPTH]
                pltpu.matmul_acc_lhs(unit, left[at, :], load_staged_rhs=load)
                waiting.append((at, m, unit))
            if len(waiting) > 2 * (DEPTH - 1):
                for _ in range(2):
                    at, m, unit = waiting.pop(0)
                    finish(at, m, pltpu.matmul_pop(unit))
        if earlier is not None:
            multiply(units, *earlier, turn)
            store(units, earlier[0])
        for at, m, unit in waiting:
            finish(at, m, pltpu.matmul_pop(unit))
        return c, lows

    def multiply(units, c, lows, part):
        turn, each = 0, count // 256 // 3
        for k in range(part * each, part * each + each):
            rows = slice(k * 256, k * 256 + 256)
            for source, which, height in ((hi_refs[c], -2, 96), (lows, -1, 64)):
                for m in range(2):
                    pltpu.matmul_push_rhs(source[rows, m * 256 : m * 256 + 256], turn % 2, m)
                for m in range(2):
                    pltpu.matmul_acc_lhs(units[m][which], pack_ref[64 : 64 + height, rows], load_staged_rhs=turn % 2)
                turn += 1

    def store(units, c):
        for m in range(2):
            cols = slice(c * TILE + m * 256, c * TILE + m * 256 + 256)
            a, b = pltpu.matmul_pop(units[m][-2]), pltpu.matmul_pop(units[m][-1])
            value = a[0:SIDES] + (a[SIDES : 2 * SIDES] + ((b[0:SIDES] + b[SIDES:]) + a[2 * SIDES :]))
            if acc_ref is not None:
                value = value + acc_ref[:, cols]
            out_ref[:, cols] = value

    def steps(*units):
        each = len(units) // 2
        units = (units[:each], units[each:])
        earlier = None
        for c in range(near, tiles):
            slot = (c - near) % KEEP
            if c >= near + KEEP:
                copy(c - KEEP, slot).wait()
            earlier = step(units, c, slot, earlier)
            copy(c, slot).start()
        for c in range(near):
            earlier = step(units, c, None, earlier)
        for part in range(3):
            multiply(units, *earlier, part)
        store(units, earlier[0])
        for c in range(max(near, tiles - KEEP), tiles):
            copy(c, (c - near) % KEEP).wait()

    heights = [ROWS] * DEPTH + [96, 64]
    pl.run_scoped(steps, *[pltpu.ACC(m)((h, 256), F32) for m in range(2) for h in heights])


def finish_tile(kind, sums, v, extra, acc_ref, tile_ref, out_ref):
    width = out_ref.shape[1] - LANES
    if kind == "own":
        tile = tile_ref[:, tile_ref.shape[1] - LANES :]
    else:
        tile = in_lanes(*sums(v, *extra))
        if acc_ref is not None:
            tile = tile + acc_ref[:, acc_ref.shape[1] - LANES :]
    out_ref[:, width:] = tile


def form(kind, near, pack, right, acc):
    count, width = pack.shape[1], right.shape[1]
    tiles = width // TILE
    outs = [pltpu.VMEM((count, TILE), BF16)] * (tiles + near)
    specs = [VM] * (tiles + near)
    scratch = [pltpu.VMEM((256, count), BF16), pltpu.VMEM((count, 256), BF16)]
    keep = min(KEEP, tiles - near)
    if keep:
        outs.append(pltpu.HBM((tiles - near, count, TILE), BF16))
        specs.append(HB)
        scratch += [pltpu.VMEM((keep, count, TILE), BF16), pltpu.SemaphoreType.DMA((keep,))]
    *parts, out = call(
        functools.partial(form_kernel, 3.0 / 64, kind, near),
        outs + [f32(SIDES, width + LANES)],
        FORM_ROOM + 3 * 2**19 * keep,
        scratch,
        cost=8.5,
        out_specs=specs + [VM],
        name="form",
    )(pack, right, *acc)
    return (parts[:tiles], parts[tiles : tiles + near], parts[tiles + near :]), out


def apply_kernel(sums, kind, columns, n_extra, all_tiles, near, *refs):
    v_ref, *refs = refs
    extra, refs = refs[:n_extra], refs[n_extra:]
    hi_refs, refs = refs[:all_tiles], refs[all_tiles:]
    near_refs, refs = refs[:near], refs[near:]
    far_ref, refs = (refs[0], refs[1:]) if near < all_tiles else (None, refs)
    acc_ref, refs = (None, refs) if kind == "first" else (refs[0], refs[1:])
    tile_ref, refs = (refs[0], refs[1:]) if kind == "own" else (None, refs)
    out_ref, parts, *own = refs
    if own:
        slots, sems = own
    tiles = range(columns // TILE, (columns + out_ref.shape[1] - LANES) // TILE)
    far_tiles = [c for c in tiles if c >= near]

    def copy(c):
        slot = c - far_tiles[0]
        return pltpu.make_async_copy(far_ref.at[c - near], slots.at[slot], sems.at[slot])

    for c in far_tiles:
        copy(c).start()
    v = v_ref[...]
    for place, part in enumerate(split3(v)):
        parts[place * SIDES : place * SIDES + SIDES, :] = part
    for c in tiles:
        cols, from_cols = (slice(at, at + TILE) for at in (c * TILE - columns, c * TILE))
        a = jnp.dot(parts[...], hi_refs[c][...], preferred_element_type=F32)
        value = a[0:SIDES] + (a[SIDES : 2 * SIDES] + a[2 * SIDES :])
        if acc_ref is not None:
            value = value + acc_ref[:, from_cols]
        out_ref[:, cols] = value
    finish_tile(kind, sums, v, extra, acc_ref, tile_ref, out_ref)
    for c in tiles:
        cols, from_cols = (slice(at, at + TILE) for at in (c * TILE - columns, c * TILE))
        if c >= near:
            copy(c).wait()
            low = slots[c - far_tiles[0]]
        else:
            low = near_refs[c][...]
        b = jnp.dot(parts[0 : 2 * SIDES, :], low, preferred_element_type=F32)
        out_ref[:, cols] = out_ref[:, cols] + (b[0:SIDES] + b[SIDES:])


def apply_block(sums, kind, columns, width, v, extra, hi, near, far, acc, tile):
    count = hi[0].shape[0]
    slots = sum(c >= len(near) for c in range(columns // TILE, (columns + width) // TILE))
    scratch = [pltpu.VMEM((3 * SIDES, count), BF16)]
    if slots:
        scratch += [pltpu.VMEM((slots, count, TILE), BF16), pltpu.SemaphoreType.DMA((slots,))]
    args, specs = [v, *extra, *hi], [VM] * (1 + len(extra) + len(hi))
    args += [*near, *[pltpu.with_memory_space_constraint(array, pltpu.HBM) for array in far]]
    specs += [VM] * len(near) + [HB] * len(far)
    return call(
        functools.partial(apply_kernel, sums, kind, columns, len(extra), len(hi), len(near)),
        [f32(SIDES, width + LANES)],
        APPLY_ROOM + 3 * 2**19 * slots,
        scratch,
        cost=(4.4 if slots else 3.2) * width / 3072,
        in_specs=specs + [VM] * len(acc + tile),
        name="apply",
    )(*args, *acc, *tile)[0]


def summed(own, other):
    fold = call(fold_kernel, [f32(SIDES, WIDTH + LANES)] * 4, 2**20, name="fold")
    parts = fold(own, swap(other, "c", 1, 2))
    return [parts[0]] + [swap(parts[m], Z, m) for m in (1, 3, 2)]


def first_product(rows, right):
    packs = [rows] + [swap(rows, "x", k) for k in (1, 3)]
    blocks, acc = [], []
    for k in range(4):
        if k == 1:
            acc[0], rows = lax.optimization_barrier((acc[0], rows))
            packs.append(swap(rows, "x", 2))
        pack = packs[k]
        block, out = form("next" if k else "first", NEAR[k], pack, right, acc)
        blocks.append(block)
        acc = [out]
    half = 4 * WIDTH
    halves = [jnp.concatenate([out[:, at : at + half], out[:, 2 * half :]], axis=1) for at in (0, half)]
    return summed(*halves), blocks, packs


def product(sums, vectors, extras, blocks, common=()):
    half, last = 4 * WIDTH, len(vectors) - 1

    def work(kind, k, columns, width, acc, tile):
        extra = [e[k] for e in extras] + list(common)
        return apply_block(sums, kind, columns, width, vectors[k], extra, *blocks[k], acc, tile)

    acc = []
    for k in range(last):
        acc = [work("next" if k else "first", k, 0, 2 * half, acc, [])]
    other = work("other", last, half, half, acc, [])
    return summed(work("own", last, 0, half, acc, [other]), other)


def fold_kernel(own_ref, got_ref, *outs):
    value = own_ref[...] + got_ref[...]
    for m, out in enumerate(outs):
        out[:, :WIDTH] = value[:, m * WIDTH : m * WIDTH + WIDTH]
        out[:, WIDTH:] = value[:, 4 * WIDTH :]


def total(a):
    return jnp.sum(a, axis=1, keepdims=True)


def in_lanes(*values):
    lane = lax.broadcasted_iota(jnp.int32, (SIDES, LANES), 1)
    tile = jnp.zeros((SIDES, LANES), F32)
    for place, value in enumerate(values):
        tile = jnp.where(lane == place, value, tile)
    return tile


def sums_first(v):
    return (total(v * v),)


def sums_second(v, b_ref):
    return total(unpacked(b_ref) * v), total(v * v)


def sums_third(v, b_ref, u0_ref, coef):
    b, u0 = unpacked(b_ref), u0_ref[...]
    r1 = b - coef[:, 0:1] * u0
    d1 = r1 + coef[:, 1:2] * b
    return total(d1 * v), total(v * v), total(r1 * v), total(r1 * r1)


def gather_plane(array):
    return round_of(jnp.concatenate(round_of(array, "y"), axis=1), "x")


def added(refs):
    got = (refs[0][...] + refs[1][...]) + (refs[2][...] + refs[3][...])
    return got[:, :WIDTH], got[:, WIDTH:]


def first_kernel(m0, m1, m2, m3, b_ref, u_ref, sums_ref):
    got, sums_ref[...] = added((m0, m1, m2, m3))
    u_ref[...] = got + SHRINKAGE * b_ref[...]


def second_kernel(m0, m1, m2, m3, b_ref, u0_ref, sums_ref, u1_ref, r1_ref, d1_ref, ar1_ref, coef_ref):
    got, sums = added((m0, m1, m2, m3))
    b, u0 = b_ref[...], u0_ref[...]
    y = got + SHRINKAGE * u0
    rr0, c0, q0 = sums_ref[:, 0:1], sums[:, 0:1], sums[:, 1:2]
    a0 = rr0 / c0
    rr1 = rr0 - 2.0 * a0 * c0 + a0 * a0 * q0
    b0 = rr1 / rr0
    r1 = b - a0 * u0
    ar1 = u0 - a0 * y
    r1_ref[...] = r1
    d1_ref[...] = r1 + b0 * b
    ar1_ref[...] = ar1
    u1_ref[...] = ar1 + b0 * u0
    coef_ref[...] = in_lanes(a0, b0)


def third_kernel(
    m0, m1, m2, m3, b_ref, u1_ref, r1_ref, d1_ref, ar1_ref, coef_ref, x2_ref, r2_ref, d2_ref, u2_ref, sums_ref
):
    got, sums = added((m0, m1, m2, m3))
    u1, d1, r1 = u1_ref[...], d1_ref[...], r1_ref[...]
    y = got + SHRINKAGE * u1
    c1, q1, p1, rr1 = (sums[:, k : k + 1] for k in range(4))
    a1 = rr1 / c1
    rr2 = rr1 - 2.0 * a1 * p1 + a1 * a1 * q1
    b1 = rr2 / rr1
    r2 = r1 - a1 * u1
    d2 = r2 + b1 * d1
    u2 = (ar1_ref[...] - a1 * y) + b1 * u1
    x2_ref[...] = coef_ref[:, 0:1] * b_ref[...] + a1 * d1
    r2_ref[...] = r2
    d2_ref[...] = d2
    u2_ref[...] = u2
    tile = jnp.concatenate([in_lanes(total(d2 * u2), total(r2 * r2)), jnp.zeros((LANES - SIDES, LANES), F32)], axis=0)
    sums_ref[...] = jnp.transpose(tile)[0:8, :]


def last_kernel(sums_ref, x2_ref, r2_ref, d2_ref, u2_ref, at_ref, x_ref, r_ref, s_ref):
    got = jnp.transpose(jnp.sum(sums_ref[...], axis=0))[0:SIDES, :]
    a2 = got[:, 1:2] / got[:, 0:1]
    x = x2_ref[...] + a2 * d2_ref[...]
    r = r2_ref[...] - a2 * u2_ref[...]
    x_ref[...] = x
    r_ref[...] = r
    place = lax.broadcasted_iota(jnp.int32, (WIDTH, LANES), 0)
    pick = jnp.where(place == at_ref[...], 1.0, 0.0).astype(BF16)
    parts = [jnp.dot(p, pick, preferred_element_type=F32) for p in split3(r + SHRINKAGE * x)]
    s_ref[...] = jnp.abs((parts[0] + parts[1]) + parts[2])


def body(points, targets, cal_offset):
    small = 4 * 2**20
    vector = f32(SIDES, WIDTH)
    tile = f32(SIDES, LANES)
    b = targets
    scratch = [pltpu.VMEM((SIDES, WIDTH), F32), pltpu.SemaphoreType.DMA((2,))]
    outs = [jax.ShapeDtypeStruct((160, WIDTH), BF16)]
    in_hbm = [pltpu.with_memory_space_constraint(array, pltpu.HBM) for array in (points, b)]
    pack = call(pack_kernel, outs, small, scratch, in_specs=[HB, HB], name="pack")(*in_hbm)[0]
    rows = jnp.concatenate(round_of(pack, "y"), axis=1)
    pair = jnp.concatenate([pack[0:64], swap(points, "c", 1, 2)], axis=1)
    pairs = [pair] + [swap(pair, Z, m) for m in (1, 2, 3)]
    xi = jnp.concatenate([p[:, :WIDTH] for p in pairs] + [p[:, WIDTH:] for p in pairs], axis=1)
    prepare = functools.partial(prepare_kernel, 3.0 / points.shape[0])
    right = call(prepare, [jax.ShapeDtypeStruct((256, xi.shape[1]), BF16)], small, name="prepare")(xi)[0]
    msgs, blocks, bj = first_product(rows, right)
    u0, sums = call(first_kernel, [vector, tile], small, name="first")(*msgs, b)
    u0j = gather_plane(u0)
    msgs = product(sums_second, u0j, [bj], blocks)
    u1, r1, d1, ar1, coef = call(second_kernel, [vector] * 4 + [tile], small, name="second")(*msgs, b, u0, sums)
    msgs = product(sums_third, gather_plane(u1), [bj, u0j], blocks, (coef,))
    x2, r2, d2, u2, part = call(third_kernel, [vector] * 4 + [f32(8, LANES)], small, name="third")(
        *msgs, b, u1, r1, d1, ar1, coef
    )
    part = part + swap(part, "c", 1, 2)
    parts = lax.all_to_all(
        jnp.broadcast_to(part[None], (64, 8, LANES)), ("x", "y", *Z), split_axis=0, concat_axis=0, tiled=True
    )
    return tuple(
        call(last_kernel, [vector, vector, tile], small, name="last")(
            parts, x2, r2, d2, u2, cal_offset.reshape(1, LANES)
        )
    )


def solution(mesh):
    grid = Mesh(mesh.devices.reshape(4, 4, 2, 2, 2), ALL)
    return jax.shard_map(
        body,
        mesh=grid,
        in_specs=(P(None, ALL), P(None, ALL), P(ALL)),
        out_specs=(P(None, ALL), P(None, ALL), P(None, ALL)),
        check_vma=False,
    )
```
